32 devices in a mesh: groups: 2 (over y), shard: 2 (over x), rep: 4 (over z), sub: 2 (over core).
Axes of the slice: x: 2, y: 2, z: 4, core: 2. Of those that a mesh axis runs over, the one named last changes fastest.
Arguments:
- master: bfloat16 [8, 2048, 7168], P(('groups', 'rep'), ('shard', 'sub')), parts along dimension 0
- train_expert: int32 [4], replicated, may hold values from 0 to 3, each once
- rollout_owner: int32 [4, 1], replicated, may hold values from 0 to 3, as said below
- hidden: bfloat16 [1664, 2, 2048], P(('groups', 'shard', 'sub')), parts along dimension 0, may hold values from -6 to 6
- routes: int32 [1664, 2], P(('groups', 'shard', 'sub')), parts along dimension 0, may hold values from 0 to 3, all different within a row
- route_weight: float32 [1664, 2], P(('groups', 'shard', 'sub')), parts along dimension 0, may hold values from 0.2 to 1
Outputs:
- rollout_codes: bfloat16 [8, 2, 2048, 7168], P(('groups', 'rep'), None, None, ('shard', 'sub')), parts along dimension 0
- mixed: bfloat16 [1664, 7168], P(('groups', 'rep'), ('shard', 'sub')), parts along dimension 0
The draws below stay inside these ranges and needn't reach their ends.
There are 2 independent parts, one for each index of `groups`. The reference program is written for one: setup_inputs(seed, part) draws one part's arguments, and reference() takes and returns one part's arrays. A program takes and returns all parts, laid end to end along the dimension named above; an argument that names none is the same for every part. Nothing has to cross between parts.
Inputs may be any that keep to these rules, and one draw needn't show every extreme that they name: `train_expert`: each expert number appears once. `rollout_owner`: no owner holds more than 2 experts, and some owner holds exactly 2. `routes`: each row names 2 different experts.
All inputs are finite; a program needn't handle non-finite values.
Results may differ from the reference program's by a relative error of at most 0.019.
Values may be sent and summed in bfloat16 or wider, within the bound.
No kernel may reach another device: no remote copies, remote signals or barrier semaphores. Data moves between devices by JAX's collectives and lax.ppermute only.
A program may use at most 192 MiB of HBM per device.

```python
import math
import jax
import jax.numpy as jnp
from jax import lax

D = 7168
FF = 2048
GROUP = 32
ROWS = 832
TOPW = 2
MOST = 2
EXPERTS = 4


def draw_master(key, part):
    key = jax.random.fold_in(key, 11)
    base_key, spread_key = jax.random.split(key)
    grouped_shape = (EXPERTS, FF // GROUP, GROUP, D)
    base_values = jax.random.normal(base_key, grouped_shape, jnp.float32)
    spread = jnp.exp(jax.random.uniform(spread_key, (EXPERTS, FF // GROUP, 1, D), jnp.float32, math.log(0.05), math.log(2.0)))
    return (base_values * spread * FF ** (-0.5)).reshape(EXPERTS, FF, D).astype(jnp.bfloat16)


def draw_rollout_owner(key, part):
    key = jax.random.fold_in(key, 23)
    order_key, slot_key, coin_key = jax.random.split(key, 3)
    expert_order = jax.random.permutation(order_key, EXPERTS).astype(jnp.int32)
    slot_order = jax.random.permutation(slot_key, EXPERTS).astype(jnp.int32)
    coins = jax.random.randint(coin_key, (EXPERTS,), 0, 2).astype(jnp.int32)
    coins = coins.at[1].set(0)

    def advance(state_pair, coin_value):
        previous_step, level_now = state_pair
        step_now = jnp.where(previous_step == 0, jnp.int32(1), coin_value)
        level_now = level_now + step_now
        return ((step_now, level_now), level_now)
    ignored, levels = lax.scan(advance, (jnp.int32(1), jnp.int32(0)), coins[1:])
    levels = jnp.concatenate([jnp.zeros((1,), jnp.int32), levels])
    owners = jnp.zeros((EXPERTS,), jnp.int32).at[expert_order].set(slot_order[levels])
    return owners.reshape(EXPERTS, 1)


def block_scale(stream_key, dims, shards, smallest, top_value):
    level, own = 1.0, jax.random.fold_in(stream_key, 6)
    for dim, shards_of in shards:
        heights = jnp.exp(jax.random.uniform(jax.random.fold_in(own, dim), (shards_of,), jnp.float32, smallest / len(shards), top_value / len(shards)))
        level = level * jnp.repeat(heights, dims[dim] // shards_of).reshape([-1 if axis == dim else 1 for axis in range(len(dims))])
    return level


def picks_of(own_key, rows, amount, top, lift):
    order = jax.random.permutation(jax.random.fold_in(own_key, 1), amount)
    boost = order
    for power in range(3):
        boost = boost * boost // amount
    boost = boost * lift // amount
    chance = jax.random.randint(jax.random.fold_in(own_key, 2), (rows, amount), 0, 4096) + boost
    fixed_rows = jax.random.permutation(jax.random.fold_in(own_key, 3), rows)[jnp.arange(amount) % rows]
    chance = jnp.where(jnp.arange(rows)[:, None] == fixed_rows[None, :], 1 << 14, chance)
    priority = chance * amount + jnp.arange(amount)
    return lax.top_k(priority.astype(jnp.int32), top)[1].astype(jnp.int32)


def centred(stream_key, dims, deviation, bound, pieces=(), kind=jnp.bfloat16):
    array = jax.random.normal(stream_key, dims, jnp.float32) * deviation
    if len(pieces) > 0:
        array = block_scale(stream_key, dims, pieces, -0.22, 0.18) * array
    return jnp.clip(array, min=-bound, max=bound).astype(kind)


def setup_inputs(seed: int = 0, part: int = 0) -> dict:
    arg_keys = jax.random.split(jax.random.key(seed), 7)
    part_keys = jax.random.split(jax.random.fold_in(arg_keys[6], part), 7)
    return {
        "master": draw_master(jax.random.fold_in(jax.random.fold_in(arg_keys[6], part), 71), part),
        "train_expert": jax.random.permutation(arg_keys[1], EXPERTS).astype(jnp.int32),
        "rollout_owner": draw_rollout_owner(jax.random.fold_in(arg_keys[6], 71), part),
        "hidden": centred(part_keys[3], (ROWS, TOPW, FF), 1.0, 6.0, ((0, 4),)),
        "routes": picks_of(part_keys[4], ROWS, EXPERTS, TOPW, 8192),
        "route_weight": jnp.clip(jnp.exp(math.log(1.0) - 1.609438 * jax.random.uniform(part_keys[5], (ROWS, TOPW), jnp.float32) ** block_scale(part_keys[5], (ROWS, TOPW), ((0, 4),), -0.2, 0.2)), 0.2, 1.0),
    }


LEVELS = 15.0
FLOOR = 0.02


def quantize(weights_block):
    row_count, col_count = weights_block.shape
    grouped = weights_block.reshape(row_count // GROUP, GROUP, col_count).astype(jnp.float32)
    lowest = jnp.min(grouped, axis=1)
    highest = jnp.max(grouped, axis=1)
    zero_point = lowest.astype(jnp.bfloat16)
    group_scale = (jnp.maximum(highest - lowest, FLOOR) / LEVELS).astype(jnp.bfloat16)
    code_values = (grouped - zero_point.astype(jnp.float32)[:, None, :]) / group_scale.astype(jnp.float32)[:, None, :]
    return code_values.astype(jnp.bfloat16).reshape(row_count, col_count), group_scale, zero_point


def restore(code_values, group_scale, zero_point):
    shape_full = code_values.shape
    grouped = code_values.reshape(shape_full[:-2] + (shape_full[-2] // GROUP, GROUP, shape_full[-1])).astype(jnp.float32)
    restored = grouped * jnp.expand_dims(group_scale.astype(jnp.float32), -2) + jnp.expand_dims(zero_point.astype(jnp.float32), -2)
    return restored.astype(jnp.bfloat16).reshape(shape_full)


def rebuild(weights_block):
    code_values, group_scale, zero_point = quantize(weights_block)
    code_values = lax.optimization_barrier(code_values)
    return code_values, restore(code_values, group_scale, zero_point)


def reference(master, train_expert, rollout_owner, hidden, routes, route_weight):
    total_experts = master.shape[0]
    all_codes, all_restored = lax.map(rebuild, master)
    labels = jnp.arange(total_experts, dtype=jnp.int32)
    owners = rollout_owner[:, 0].astype(jnp.int32)
    same_owner = owners[:, None] == owners[None, :]
    ranking = jnp.sum((same_owner & (labels[None, :] < labels[:, None])).astype(jnp.int32), axis=1)
    position_of = jnp.sum(jnp.where(train_expert[None, :] == labels[:, None], labels[None, :], 0), axis=1).astype(jnp.int32)
    slot_labels = jnp.arange(MOST, dtype=jnp.int32)
    matched = (owners[:, None, None] == labels[None, :, None]) & (ranking[:, None, None] == slot_labels[None, None, :])
    present = jnp.any(matched, axis=0)
    source = jnp.sum(jnp.where(matched, position_of[:, None, None], 0), axis=0).astype(jnp.int32)
    picked = jnp.take(all_codes, source.reshape(-1), axis=0).reshape((total_experts, MOST) + all_codes.shape[1:])
    rollout_codes = jnp.where(present[:, :, None, None], picked, jnp.zeros((), jnp.bfloat16))

    def add_expert(total_sum, position):
        expert_id = train_expert[position]
        weight_here = jnp.where(routes == expert_id, route_weight, jnp.zeros((), jnp.float32))
        combined = jnp.sum(weight_here[:, :, None] * hidden.astype(jnp.float32), axis=1).astype(jnp.bfloat16)
        block_here = lax.dynamic_index_in_dim(all_restored, position, 0, keepdims=False)
        return total_sum + jnp.dot(combined, block_here, preferred_element_type=jnp.float32), None

    start_sum = jnp.zeros((hidden.shape[0], master.shape[2]), jnp.float32)
    total_sum, ignored = lax.scan(add_expert, start_sum, labels)
    return rollout_codes, total_sum.astype(jnp.bfloat16)
```

```python
import functools
import itertools

import jax
import jax.numpy as jnp
import numpy as np
from jax import lax
from jax.experimental import pallas as pl
from jax.experimental.pallas import tpu as pltpu
from jax.sharding import PartitionSpec as P

GROUP = 32
MOST = 2


LEVELS = 15.0
FLOOR = 0.02


def quantize(weights_block):
    row_count, col_count = weights_block.shape
    grouped = weights_block.reshape(row_count // GROUP, GROUP, col_count).astype(jnp.float32)
    lowest = jnp.min(grouped, axis=1)
    highest = jnp.max(grouped, axis=1)
    zero_point = lowest.astype(jnp.bfloat16)
    group_scale = (jnp.maximum(highest - lowest, FLOOR) / LEVELS).astype(jnp.bfloat16)
    code_values = (grouped - zero_point.astype(jnp.float32)[:, None, :]) / group_scale.astype(
        jnp.float32
    )[:, None, :]
    return (code_values.astype(jnp.bfloat16).reshape(row_count, col_count), group_scale, zero_point)


def restore(code_values, group_scale, zero_point):
    shape_full = code_values.shape
    grouped = code_values.reshape(
        shape_full[:-2] + (shape_full[-2] // GROUP, GROUP, shape_full[-1])
    ).astype(jnp.float32)
    restored = grouped * jnp.expand_dims(group_scale.astype(jnp.float32), -2) + jnp.expand_dims(
        zero_point.astype(jnp.float32), -2
    )
    return restored.astype(jnp.bfloat16).reshape(shape_full)


def local_slots(train_expert, rollout_owner, owner_index):
    total_experts = train_expert.shape[0]
    owners = rollout_owner[:, 0]
    labels = jnp.arange(total_experts, dtype=jnp.int32)
    same_owner = owners[:, None] == owners[None, :]
    ranking = jnp.sum((same_owner & (labels[None, :] < labels[:, None])).astype(jnp.int32), axis=1)
    own_mask = owners == owner_index
    chosen = []
    for slot_index in range(MOST):
        matched = own_mask & (ranking == slot_index)
        present = jnp.any(matched)
        expert_id = jnp.where(present, jnp.sum(jnp.where(matched, labels, 0)), -1)
        position = jnp.sum(jnp.where(train_expert == expert_id, labels, 0))
        chosen.append((expert_id, position, present))
    return chosen


def fold_select(chosen, selected, pieces, first_index):
    span = pieces[0].shape[0]
    result = []
    for member, held in zip(pieces, selected):
        layers = []
        for slot_index in range(MOST):
            expert_id, position, present = chosen[slot_index]
            inside = present & (position >= first_index) & (position < first_index + span)
            offset = jnp.clip(position, 0, span - 1)
            taken = lax.dynamic_index_in_dim(member, offset, 0, keepdims=False)
            layers.append(jnp.where(inside, taken, held[slot_index]))
        result.append(jnp.stack(layers))
    return tuple(result)


def general_body(master, train_expert, rollout_owner, hidden, routes, route_weight):
    local_rows = master[0]
    owner_index = lax.axis_index("rep")
    chosen = local_slots(train_expert, rollout_owner, owner_index)
    code_values, group_scale, zero_point = quantize(local_rows)
    relaid = (
        lax.all_to_all(code_values, ("shard", "sub"), split_axis=1, concat_axis=0, tiled=True),
        lax.all_to_all(group_scale, ("shard", "sub"), split_axis=1, concat_axis=0, tiled=True),
        lax.all_to_all(zero_point, ("shard", "sub"), split_axis=1, concat_axis=0, tiled=True),
    )
    start_slots = tuple((jnp.zeros((MOST,) + member.shape, member.dtype) for member in relaid))
    gathered = fold_select(
        chosen,
        start_slots,
        (
            lax.all_gather(relaid[0][None], "rep", axis=0, tiled=True),
            lax.all_gather(relaid[1][None], "rep", axis=0, tiled=True),
            lax.all_gather(relaid[2][None], "rep", axis=0, tiled=True),
        ),
        jnp.int32(0),
    )
    slot_codes = gathered[0]
    slot_values = restore(gathered[0], gathered[1], gathered[2])
    blended_list = []
    for slot_index in range(MOST):
        expert_id = chosen[slot_index][0]
        weight_here = jnp.where(routes == expert_id, route_weight, jnp.zeros((), jnp.float32))
        blended_list.append(jnp.sum(weight_here[:, :, None] * hidden, axis=1).astype(jnp.bfloat16))
    blended = jnp.stack(blended_list)
    all_blended = lax.all_gather(blended, ("shard", "sub"), axis=1, tiled=True)
    mixed = lax.psum_scatter(
        jnp.einsum("srf,sfd->rd", all_blended, slot_values, preferred_element_type=jnp.float32),
        "rep",
        scatter_dimension=0,
        tiled=True,
    ).astype(jnp.bfloat16)
    return (slot_codes[None], mixed)


CELL = ("shard", "sub")
VMEM_BYTES = 48 * 1024 * 1024


def routing_maps(reps):
    return [
        owners
        for owners in itertools.product(range(reps), repeat=reps)
        if max(owners.count(r) for r in range(reps)) <= MOST
    ]


def map_rounds(owners):
    rounds = [[] for _ in range(MOST)]
    for position, owner in enumerate(owners):
        if owner != position:
            taken = sum(owners[q] == owner and q != owner for q in range(position))
            rounds[taken].append((position, owner))
    return rounds


def routing(train_expert, rollout_owner, rep):
    reps = train_expert.shape[0]
    owners = jnp.take(rollout_owner[:, 0], train_expert)
    table = np.zeros((reps**reps,), np.int32)
    for index, owners_of in enumerate(routing_maps(reps)):
        table[sum(owner * reps**p for p, owner in enumerate(owners_of))] = index
    number = jnp.sum(owners * jnp.asarray([reps**p for p in range(reps)], jnp.int32))
    which = jnp.asarray(table)[number]
    positions = jnp.arange(reps, dtype=jnp.int32)
    sources = []
    for unused, position, present in local_slots(train_expert, rollout_owner, rep):
        earlier = jnp.sum(((owners == rep) & (positions != rep) & (positions < position)).astype(jnp.int32))
        source = jnp.where(position == rep, 0, 1 + earlier)
        sources.append(jnp.where(present, source, MOST + 1))
    return which, jnp.stack(sources).astype(jnp.int32)


def group_values(block):
    values = block.astype(jnp.float32)
    lowest = jnp.min(values, axis=0, keepdims=True)
    highest = jnp.max(values, axis=0, keepdims=True)
    scale = (jnp.maximum(highest - lowest, FLOOR) / LEVELS).astype(jnp.bfloat16).astype(jnp.float32)
    codes = ((values - lowest) * (1.0 / scale)).astype(jnp.bfloat16)
    return codes, scale, lowest


def cut_kernel(scalars, master_ref, piece_ref):
    piece_ref[...] = master_ref[...]


def cut(scalars, master, step, cells):
    rows, width = master.shape[0], master.shape[1] // cells
    tile = rows // 4
    return pl.pallas_call(
        cut_kernel,
        grid_spec=pltpu.PrefetchScalarGridSpec(
            num_scalar_prefetch=1,
            grid=(4,),
            in_specs=[pl.BlockSpec((tile, width), lambda i, scalars: (i, scalars[0] ^ step))],
            out_specs=pl.BlockSpec((tile, width), lambda i, scalars: (i, 0)),
        ),
        out_shape=jax.ShapeDtypeStruct((rows, width), master.dtype),
        cost_estimate=pl.CostEstimate(flops=0, bytes_accessed=4 * rows * width, transcendentals=0),
        name=f"cut_{step}",
    )(scalars, master)


def mix_kernel(cells, scalars, *refs):
    pieces, blends, outs = refs[:cells], refs[cells : 2 * cells], refs[2 * cells : 3 * cells]
    combined, restored = refs[3 * cells :]
    me, rep = scalars[0], scalars[1]
    span, chunk = pieces[0].shape[0], blends[0].shape[0]

    @pl.when(pl.program_id(0) == 0)
    def _():
        for step in range(cells):
            place = lax.rem((me ^ step) - rep + cells, cells)
            combined[pl.ds(pl.multiple_of(place * chunk, 16), chunk), :] = blends[step][...]

    for step in range(cells):
        first = (me ^ step) * span

        def group(g, carry, step=step, first=first):
            codes, scale, lowest = group_values(pieces[step][pl.ds(pl.multiple_of(g * GROUP, GROUP), GROUP), :])
            value = codes.astype(jnp.float32) * scale + lowest
            restored[pl.ds(pl.multiple_of(first + g * GROUP, GROUP), GROUP), :] = value.astype(jnp.bfloat16)
            return carry

        lax.fori_loop(0, span // GROUP, group, 0, unroll=8)
    total = jnp.dot(combined[...], restored[...], preferred_element_type=jnp.float32)
    for ahead in range(cells):
        outs[ahead][...] = total[ahead * chunk : (ahead + 1) * chunk].astype(outs[ahead].dtype)


def mix(scalars, pieces, blends):
    cells = len(pieces)
    span, width = pieces[0].shape
    chunk, depth = blends[0].shape
    tile = 256
    return pl.pallas_call(
        functools.partial(mix_kernel, cells),
        grid_spec=pltpu.PrefetchScalarGridSpec(
            num_scalar_prefetch=1,
            grid=(width // tile,),
            in_specs=[pl.BlockSpec((span, tile), lambda i, scalars: (0, i))] * cells
            + [pl.BlockSpec((chunk, depth), lambda i, scalars: (0, 0))] * cells,
            out_specs=[pl.BlockSpec((chunk, tile), lambda i, scalars: (0, i))] * cells,
            scratch_shapes=[
                pltpu.VMEM((cells * chunk, depth), jnp.bfloat16),
                pltpu.VMEM((depth, tile), jnp.bfloat16),
            ],
        ),
        out_shape=[jax.ShapeDtypeStruct((chunk, width), jnp.bfloat16)] * cells,
        compiler_params=pltpu.CompilerParams(vmem_limit_bytes=VMEM_BYTES),
        cost_estimate=pl.CostEstimate(
            flops=2 * cells * chunk * depth * width,
            bytes_accessed=2 * (depth * width + cells * chunk * (depth + width)),
            transcendentals=0,
        ),
        name="mix",
    )(scalars, *pieces, *blends)


def code_kernel(held, scalars, *refs):
    sources, out_ref = refs[:held], refs[-1]
    source = scalars[2 + pl.program_id(0)]
    for k in range(held):

        @pl.when(source == k)
        def _(k=k):
            def group(g, carry):
                rows = pl.ds(pl.multiple_of(g * GROUP, GROUP), GROUP)
                out_ref[0, 0, rows, :] = group_values(sources[k][rows, :])[0]
                return carry

            lax.fori_loop(0, out_ref.shape[2] // GROUP, group, 0, unroll=2)

    @pl.when(source == held)
    def _():
        out_ref[...] = jnp.zeros_like(out_ref)


def code(scalars, step, sources, so_far, depth):
    held = len(sources)
    span, width = sources[0].shape
    tiles = 4
    tile = span // tiles

    def source_map(k):
        def index(slot, t, scalars):
            before = jnp.where((slot > 0) & (scalars[2] == k), tiles - 1, 0)
            return jnp.where(scalars[2 + slot] == k, t, before), 0

        return index

    first = so_far is None
    return pl.pallas_call(
        functools.partial(code_kernel, held),
        grid_spec=pltpu.PrefetchScalarGridSpec(
            num_scalar_prefetch=1,
            grid=(MOST, tiles),
            in_specs=[pl.BlockSpec((tile, width), source_map(k)) for k in range(held)]
            + ([] if first else [pl.BlockSpec(memory_space=pl.ANY)]),
            out_specs=pl.BlockSpec(
                (1, 1, tile, width), lambda slot, t, scalars: (0, slot, (scalars[0] ^ step) * tiles + t, 0)
            ),
        ),
        out_shape=jax.ShapeDtypeStruct((1, MOST, depth, width), jnp.bfloat16),
        input_output_aliases={} if first else {1 + held: 0},
        compiler_params=pltpu.CompilerParams(vmem_limit_bytes=VMEM_BYTES),
        cost_estimate=pl.CostEstimate(
            flops=8 * MOST * span * width, bytes_accessed=4 * MOST * span * width, transcendentals=0
        ),
        name=f"code_{step}",
    )(scalars, *sources, *([] if first else [so_far]))


def routed_body(cells, master, train_expert, rollout_owner, hidden, routes, route_weight):
    local_rows = master[0]
    reps = train_expert.shape[0]
    rep = lax.axis_index("rep")
    cell = lax.axis_index(CELL)
    which, slot_source = routing(train_expert, rollout_owner, rep)
    scalars = jnp.concatenate([jnp.stack([cell, rep]).astype(jnp.int32), slot_source])

    def swap(array, step):
        return lax.ppermute(array, CELL, [(c, c ^ step) for c in range(cells)])

    pieces = [cut(scalars, local_rows, step, cells) for step in range(cells)]
    pieces = [pieces[0]] + [swap(pieces[step], step) for step in range(1, cells)]

    weight_here = jnp.where(routes == train_expert[rep], route_weight, jnp.zeros((), jnp.float32))
    blend = jnp.sum(weight_here[:, :, None] * hidden, axis=1).astype(jnp.bfloat16)
    blends = [blend] + [swap(blend, step) for step in range(1, cells)]

    def mover(owners):
        def move(*blocks):
            return tuple(
                tuple(lax.ppermute(block, "rep", pairs) for pairs in map_rounds(owners)) for block in blocks
            )

        return move

    movers = [mover(owners) for owners in routing_maps(reps)]
    half = cells // 2
    arrived = lax.switch(which, movers, *pieces[:half]) + lax.switch(which, movers, *pieces[half:])

    terms = mix(scalars, pieces, blends)
    total = terms[0].astype(jnp.float32)
    for ahead in range(1, reps):
        total += lax.ppermute(terms[ahead], "rep", [(r, (r + ahead) % reps) for r in range(reps)]).astype(jnp.float32)
    codes = None
    for step in range(cells):
        codes = code(scalars, step, (pieces[step],) + arrived[step], codes, cells * local_rows.shape[0])
    return codes, total.astype(jnp.bfloat16)


def solution(mesh):
    in_specs = (
        P(("groups", "rep"), ("shard", "sub"), None),
        P(),
        P(),
        P(("groups", "shard", "sub"), None, None),
        P(("groups", "shard", "sub"), None),
        P(("groups", "shard", "sub"), None),
    )
    out_specs = (
        P(("groups", "rep"), None, None, ("shard", "sub")),
        P(("groups", "rep"), ("shard", "sub")),
    )
    cells = mesh.shape["shard"] * mesh.shape["sub"]
    reps = mesh.shape["rep"]

    def body(master, *rest):
        rows, columns = master.shape[1:]
        fits = reps == cells == 4 and rows % (4 * GROUP) == 0 and columns % (cells * 256) == 0
        if fits:
            return routed_body(cells, master, *rest)
        return general_body(master, *rest)

    return jax.shard_map(body, mesh=mesh, in_specs=in_specs, out_specs=out_specs, check_vma=False)
```

```python
import functools
import itertools

import jax
import jax.numpy as jnp
import numpy as np
from jax import lax
from jax.experimental import pallas as pl
from jax.experimental.pallas import tpu as pltpu
from jax.sharding import PartitionSpec as P

GROUP = 32
MOST = 2


LEVELS = 15.0
FLOOR = 0.02


def quantize(weights_block):
    row_count, col_count = weights_block.shape
    grouped = weights_block.reshape(row_count // GROUP, GROUP, col_count).astype(jnp.float32)
    lowest = jnp.min(grouped, axis=1)
    highest = jnp.max(grouped, axis=1)
    zero_point = lowest.astype(jnp.bfloat16)
    group_scale = (jnp.maximum(highest - lowest, FLOOR) / LEVELS).astype(jnp.bfloat16)
    code_values = (grouped - zero_point.astype(jnp.float32)[:, None, :]) / group_scale.astype(
        jnp.float32
    )[:, None, :]
    return (code_values.astype(jnp.bfloat16).reshape(row_count, col_count), group_scale, zero_point)


def restore(code_values, group_scale, zero_point):
    shape_full = code_values.shape
    grouped = code_values.reshape(
        shape_full[:-2] + (shape_full[-2] // GROUP, GROUP, shape_full[-1])
    ).astype(jnp.float32)
    restored = grouped * jnp.expand_dims(group_scale.astype(jnp.float32), -2) + jnp.expand_dims(
        zero_point.astype(jnp.float32), -2
    )
    return restored.astype(jnp.bfloat16).reshape(shape_full)


def local_slots(train_expert, rollout_owner, owner_index):
    total_experts = train_expert.shape[0]
    owners = rollout_owner[:, 0]
    labels = jnp.arange(total_experts, dtype=jnp.int32)
    same_owner = owners[:, None] == owners[None, :]
    ranking = jnp.sum((same_owner & (labels[None, :] < labels[:, None])).astype(jnp.int32), axis=1)
    own_mask = owners == owner_index
    chosen = []
    for slot_index in range(MOST):
        matched = own_mask & (ranking == slot_index)
        present = jnp.any(matched)
        expert_id = jnp.where(present, jnp.sum(jnp.where(matched, labels, 0)), -1)
        position = jnp.sum(jnp.where(train_expert == expert_id, labels, 0))
        chosen.append((expert_id, position, present))
    return chosen


def fold_select(chosen, selected, pieces, first_index):
    span = pieces[0].shape[0]
    result = []
    for member, held in zip(pieces, selected):
        layers = []
        for slot_index in range(MOST):
            expert_id, position, present = chosen[slot_index]
            inside = present & (position >= first_index) & (position < first_index + span)
            offset = jnp.clip(position, 0, span - 1)
            taken = lax.dynamic_index_in_dim(member, offset, 0, keepdims=False)
            layers.append(jnp.where(inside, taken, held[slot_index]))
        result.append(jnp.stack(layers))
    return tuple(result)


def general_body(master, train_expert, rollout_owner, hidden, routes, route_weight):
    local_rows = master[0]
    owner_index = lax.axis_index("rep")
    chosen = local_slots(train_expert, rollout_owner, owner_index)
    code_values, group_scale, zero_point = quantize(local_rows)
    relaid = (
        lax.all_to_all(code_values, ("shard", "sub"), split_axis=1, concat_axis=0, tiled=True),
        lax.all_to_all(group_scale, ("shard", "sub"), split_axis=1, concat_axis=0, tiled=True),
        lax.all_to_all(zero_point, ("shard", "sub"), split_axis=1, concat_axis=0, tiled=True),
    )
    start_slots = tuple((jnp.zeros((MOST,) + member.shape, member.dtype) for member in relaid))
    gathered = fold_select(
        chosen,
        start_slots,
        (
            lax.all_gather(relaid[0][None], "rep", axis=0, tiled=True),
            lax.all_gather(relaid[1][None], "rep", axis=0, tiled=True),
            lax.all_gather(relaid[2][None], "rep", axis=0, tiled=True),
        ),
        jnp.int32(0),
    )
    slot_codes = gathered[0]
    slot_values = restore(gathered[0], gathered[1], gathered[2])
    blended_list = []
    for slot_index in range(MOST):
        expert_id = chosen[slot_index][0]
        weight_here = jnp.where(routes == expert_id, route_weight, jnp.zeros((), jnp.float32))
        blended_list.append(jnp.sum(weight_here[:, :, None] * hidden, axis=1).astype(jnp.bfloat16))
    blended = jnp.stack(blended_list)
    all_blended = lax.all_gather(blended, ("shard", "sub"), axis=1, tiled=True)
    mixed = lax.psum_scatter(
        jnp.einsum("srf,sfd->rd", all_blended, slot_values, preferred_element_type=jnp.float32),
        "rep",
        scatter_dimension=0,
        tiled=True,
    ).astype(jnp.bfloat16)
    return (slot_codes[None], mixed)


CELL = ("shard", "sub")
VMEM_BYTES = 48 * 1024 * 1024
ROUNDS = 2
TILES = 4
CODE_WEIGHT = 1


def moves(owners):
    return frozenset((p, owner) for p, owner in enumerate(owners) if owner != p)


def top_load(pairs, reps):
    return max(
        sum(low <= link < high for low, high in way)
        for way in ([(a, b) for a, b in pairs], [(b, a) for a, b in pairs])
        for link in range(reps - 1)
    )


def in_rounds(pairs):
    rounds = [[] for _ in range(ROUNDS)]

    def place(rest):
        if not rest:
            return True
        source, target = rest[0]
        for chosen in rounds:
            if all(source != a and target != b for a, b in chosen):
                chosen.append(rest[0])
                if place(rest[1:]):
                    return True
                chosen.pop()
        return False

    return rounds if place(sorted(pairs)) else None


@functools.lru_cache(maxsize=None)
def plans(reps):
    maps = [
        owners
        for owners in itertools.product(range(reps), repeat=reps)
        if max(owners.count(r) for r in range(reps)) <= MOST
    ]
    pairs = [(a, b) for a in range(reps) for b in range(reps) if a != b]
    chosen, table = [], np.zeros((reps**reps,), np.int32)
    for load in range(1, reps):
        todo = sorted(o for o in maps if max(1, top_load(moves(o), reps)) == load)
        if not todo:
            continue
        fitting = []
        for bits in range(1 << len(pairs)):
            subset = frozenset(pair for i, pair in enumerate(pairs) if bits >> i & 1)
            degrees = [sum(pair[side] == r for pair in subset) for side in (0, 1) for r in range(reps)]
            if max(degrees) <= ROUNDS and top_load(subset, reps) <= load:
                fitting.append(subset)
        while todo:
            best = max(fitting, key=lambda s: (sum(moves(o) <= s for o in todo), -len(s), sorted(s)))
            for owners in todo:
                if moves(owners) <= best:
                    table[sum(owner * reps**p for p, owner in enumerate(owners))] = len(chosen)
            todo = [o for o in todo if not moves(o) <= best]
            chosen.append(in_rounds(best))
    return chosen, table


def route_kernel(reps, train_ref, owner_ref, table_ref, round_ref, out_ref):
    rep = lax.axis_index("rep")
    cell = lax.axis_index(CELL)
    experts = [train_ref[p] for p in range(reps)]
    owners = [owner_ref[experts[p]] for p in range(reps)]
    number = sum(owners[p] * reps**p for p in range(reps))
    plan = table_ref[number]
    out_ref[0] = cell
    out_ref[1] = rep
    for slot in range(MOST):
        out_ref[2 + slot] = ROUNDS + 1
    for p in range(reps):
        rank = sum(
            ((owners[q] == owners[p]) & (experts[q] < experts[p])).astype(jnp.int32) for q in range(reps) if q != p
        )
        source = jnp.where(rep == p, 0, ROUNDS)
        for r in range(ROUNDS - 1):
            held = round_ref[(plan * ROUNDS + r) * reps + rep]
            source = jnp.where((rep != p) & (held == p), 1 + r, source)
        for slot in range(MOST):
            here = (owners[p] == rep) & (rank == slot)
            out_ref[2 + slot] = jnp.where(here, source, out_ref[2 + slot])
    out_ref[2 + MOST] = plan
    out_ref[3 + MOST] = train_ref[rep]


def route(train_expert, rollout_owner):
    reps = train_expert.shape[0]
    chosen, table = plans(reps)
    arrivals = np.full((len(chosen), ROUNDS, reps), -1, np.int32)
    for index, rounds in enumerate(chosen):
        for r, pairs in enumerate(rounds):
            for source, target in pairs:
                arrivals[index, r, target] = source
    smem = pl.BlockSpec(memory_space=pltpu.SMEM)
    return pl.pallas_call(
        functools.partial(route_kernel, reps),
        in_specs=[smem] * 4,
        out_specs=smem,
        out_shape=jax.ShapeDtypeStruct((4 + MOST,), jnp.int32),
        name="route",
    )(train_expert, rollout_owner[:, 0], jnp.asarray(table), jnp.asarray(arrivals.reshape(-1)))


def group_values(block):
    values = block.astype(jnp.float32)
    lowest = jnp.min(values, axis=0, keepdims=True)
    highest = jnp.max(values, axis=0, keepdims=True)
    scale = (jnp.maximum(highest - lowest, FLOOR) / LEVELS).astype(jnp.bfloat16).astype(jnp.float32)
    codes = ((values - lowest) * (1.0 / scale)).astype(jnp.bfloat16)
    return codes, scale, lowest


def copy_kernel(scalars, *refs):
    count = 1 if len(refs) == 2 else 2
    for source_ref, out_ref in zip(refs[:count], refs[-count:]):
        out_ref[...] = source_ref[...]


def column_cost(rows, width):
    return pl.CostEstimate(flops=0, bytes_accessed=8 * rows * width, transcendentals=0)


def cut(scalars, master, cells):
    rows, width = master.shape[0], master.shape[1] // cells
    tile = rows // TILES
    return pl.pallas_call(
        copy_kernel,
        grid_spec=pltpu.PrefetchScalarGridSpec(
            num_scalar_prefetch=1,
            grid=(2, TILES),
            in_specs=[pl.BlockSpec((tile, width), lambda h, t, scalars: (t, scalars[0] ^ (1 + 2 * h)))],
            out_specs=[pl.BlockSpec((tile, width), lambda h, t, scalars: (h * TILES + t, 0))],
        ),
        out_shape=[jax.ShapeDtypeStruct((2 * rows, width), master.dtype)],
        compiler_params=pltpu.CompilerParams(vmem_limit_bytes=VMEM_BYTES),
        cost_estimate=column_cost(rows, width),
        name="cut",
    )(scalars, master)[0]


def join(scalars, master, other, cells):
    rows, width = master.shape[0], master.shape[1] // cells
    tile = rows // TILES
    shapes = [jax.ShapeDtypeStruct((2 * rows, width), master.dtype)] * 2
    own = pl.pallas_call(
        copy_kernel,
        grid_spec=pltpu.PrefetchScalarGridSpec(
            num_scalar_prefetch=1,
            grid=(TILES,),
            in_specs=[
                pl.BlockSpec((tile, width), lambda t, scalars: (t, scalars[0])),
                pl.BlockSpec((tile, width), lambda t, scalars: (t, scalars[0] ^ 2)),
            ],
            out_specs=[pl.BlockSpec((tile, width), lambda t, scalars: (t, 0))] * 2,
        ),
        out_shape=shapes,
        compiler_params=pltpu.CompilerParams(vmem_limit_bytes=VMEM_BYTES),
        cost_estimate=column_cost(rows, width),
        name="join_own",
    )(scalars, master, master)
    return pl.pallas_call(
        copy_kernel,
        grid_spec=pltpu.PrefetchScalarGridSpec(
            num_scalar_prefetch=1,
            grid=(TILES,),
            in_specs=[
                pl.BlockSpec((tile, width), lambda t, scalars: (t, 0)),
                pl.BlockSpec((tile, width), lambda t, scalars: (TILES + t, 0)),
                pl.BlockSpec(memory_space=pl.ANY),
                pl.BlockSpec(memory_space=pl.ANY),
            ],
            out_specs=[pl.BlockSpec((tile, width), lambda t, scalars: (TILES + t, 0))] * 2,
        ),
        out_shape=shapes,
        input_output_aliases={3: 0, 4: 1},
        compiler_params=pltpu.CompilerParams(vmem_limit_bytes=VMEM_BYTES),
        cost_estimate=column_cost(rows, width),
        name="join_other",
    )(scalars, other, other, *own)


def mix_kernel(cells, scalars, *refs):
    halves, blends = refs[:2], refs[2 : 2 + cells]
    away_ref, keep_ref, combined, restored = refs[2 + cells :]
    me, rep = scalars[0], scalars[1]
    span, chunk = halves[0].shape[0] // 2, blends[0].shape[0]
    mate = rep ^ 1

    @pl.when(pl.program_id(0) == 0)
    def _():
        for step in range(cells):
            target = me ^ step
            place = jnp.where(target == mate, 0, jnp.where(target == 3 - mate, 1, jnp.where(target == rep, 2, 3)))
            combined[pl.ds(pl.multiple_of(place * chunk, 16), chunk), :] = blends[step][...]

    for step in range(cells):
        first = (me ^ step) * span

        def group(g, carry, step=step, first=first):
            rows = pl.ds(pl.multiple_of(step % 2 * span + g * GROUP, GROUP), GROUP)
            codes, scale, lowest = group_values(halves[step // 2][rows, :])
            value = codes.astype(jnp.float32) * scale + lowest
            restored[pl.ds(pl.multiple_of(first + g * GROUP, GROUP), GROUP), :] = value.astype(jnp.bfloat16)
            return carry

        lax.fori_loop(0, span // GROUP, group, 0, unroll=4)
    total = jnp.dot(combined[...], restored[...], preferred_element_type=jnp.float32)
    away_ref[...] = total[: 2 * chunk].astype(away_ref.dtype)
    keep_ref[...] = total[2 * chunk :].astype(keep_ref.dtype)


def mix(scalars, halves, blends):
    cells = len(blends)
    rows, width = halves[0].shape
    chunk, depth = blends[0].shape
    tile = 256
    return pl.pallas_call(
        functools.partial(mix_kernel, cells),
        grid_spec=pltpu.PrefetchScalarGridSpec(
            num_scalar_prefetch=1,
            grid=(width // tile,),
            in_specs=[pl.BlockSpec((rows, tile), lambda i, scalars: (0, i))] * 2
            + [pl.BlockSpec((chunk, depth), lambda i, scalars: (0, 0))] * cells,
            out_specs=[pl.BlockSpec((2 * chunk, tile), lambda i, scalars: (0, i))] * 2,
            scratch_shapes=[
                pltpu.VMEM((cells * chunk, depth), jnp.bfloat16),
                pltpu.VMEM((depth, tile), jnp.bfloat16),
            ],
        ),
        out_shape=[jax.ShapeDtypeStruct((2 * chunk, width), jnp.bfloat16)] * 2,
        compiler_params=pltpu.CompilerParams(vmem_limit_bytes=VMEM_BYTES),
        cost_estimate=pl.CostEstimate(
            flops=2 * cells * chunk * depth * width,
            bytes_accessed=2 * (depth * width + cells * chunk * (depth + width)),
            transcendentals=0,
        ),
        name="mix",
    )(scalars, *halves, *blends)


def code_kernel(held, scalars, *refs):
    sources, out_ref, block = refs[:held], refs[-2], refs[-1]
    source = scalars[2 + pl.program_id(0)]
    for k in range(held):

        @pl.when(source == k)
        def _(k=k):
            block[...] = sources[k][...]

    @pl.when(source < held)
    def _():
        def group(g, carry):
            rows = pl.ds(pl.multiple_of(g * GROUP, GROUP), GROUP)
            out_ref[0, 0, rows, :] = group_values(block[rows, :])[0]
            return carry

        lax.fori_loop(0, out_ref.shape[2] // GROUP, group, 0)

    @pl.when(source == held)
    def _():
        out_ref[...] = jnp.zeros_like(out_ref)


def code(scalars, half, sources, so_far, depth):
    held = len(sources)
    rows, width = sources[0].shape
    tiles = 2 * TILES
    tile = rows // tiles

    def source_map(k):
        def index(slot, t, scalars):
            before = jnp.where((slot > 0) & (scalars[2] == k), tiles - 1, 0)
            return jnp.where(scalars[2 + slot] == k, t, before), 0

        return index

    def out_map(slot, t, scalars):
        return 0, slot, (scalars[0] ^ (2 * half + t // TILES)) * TILES + t % TILES, 0

    first = so_far is None
    return pl.pallas_call(
        functools.partial(code_kernel, held),
        grid_spec=pltpu.PrefetchScalarGridSpec(
            num_scalar_prefetch=1,
            grid=(MOST, tiles),
            in_specs=[pl.BlockSpec((tile, width), source_map(k)) for k in range(held)]
            + ([] if first else [pl.BlockSpec(memory_space=pl.ANY)]),
            out_specs=pl.BlockSpec((1, 1, tile, width), out_map),
            scratch_shapes=[pltpu.VMEM((tile, width), jnp.bfloat16)],
        ),
        out_shape=jax.ShapeDtypeStruct((1, MOST, depth, width), jnp.bfloat16),
        input_output_aliases={} if first else {1 + held: 0},
        compiler_params=pltpu.CompilerParams(vmem_limit_bytes=VMEM_BYTES),
        cost_estimate=pl.CostEstimate(
            flops=8 * MOST * rows * width, bytes_accessed=4 * MOST * rows * width * CODE_WEIGHT, transcendentals=0
        ),
        name=f"code_{half}",
    )(scalars, *sources, *([] if first else [so_far]))


def routed_body(cells, master, train_expert, rollout_owner, hidden, routes, route_weight):
    local_rows = master[0]
    reps = train_expert.shape[0]
    depth = cells * local_rows.shape[0]
    scalars = route(train_expert, rollout_owner)

    def swap(array, step):
        return lax.ppermute(array, CELL, [(c, c ^ step) for c in range(cells)])

    weight_here = jnp.where(routes == scalars[3 + MOST], route_weight, jnp.zeros((), jnp.float32))
    blend = jnp.sum(weight_here[:, :, None] * hidden, axis=1).astype(jnp.bfloat16)
    near, beyond = join(scalars, local_rows, swap(cut(scalars, local_rows, cells), 1), cells)

    def planned(rounds):
        def to_owners(block):
            return tuple(lax.ppermute(block, "rep", pairs) for pairs in rounds)

        def branch(scalars, near, beyond, blend):
            near_arrived = to_owners(near)
            far = swap(beyond, 2)
            beside, across = swap(blend, 1), swap(blend, 2)
            across, far, near_arrived = lax.optimization_barrier((across, far, near_arrived))
            blends = [blend, beside, across, swap(across, 1)]
            far_arrived = to_owners(far)
            codes = code(scalars, 0, (near,) + near_arrived, None, depth)
            away, keep = mix(scalars, (near, far), blends)
            pair = keep.astype(jnp.float32) + lax.ppermute(
                away, "rep", [(r, r ^ 1) for r in range(reps)]
            ).astype(jnp.float32)
            chunk = pair.shape[0] // 2
            rest = lax.ppermute(
                pair[chunk:].astype(jnp.bfloat16), "rep", [(r, reps - 1 - r) for r in range(reps)]
            )
            mixed = (pair[:chunk] + rest.astype(jnp.float32)).astype(jnp.bfloat16)
            return mixed, codes, (far,) + far_arrived

        return branch

    mixed, codes, last = lax.switch(
        scalars[2 + MOST],
        [planned(rounds) for rounds in plans(reps)[0]],
        scalars,
        near,
        beyond,
        blend,
    )
    return code(scalars, 1, last, codes, depth), mixed


def solution(mesh):
    in_specs = (
        P(("groups", "rep"), ("shard", "sub"), None),
        P(),
        P(),
        P(("groups", "shard", "sub"), None, None),
        P(("groups", "shard", "sub"), None),
        P(("groups", "shard", "sub"), None),
    )
    out_specs = (
        P(("groups", "rep"), None, None, ("shard", "sub")),
        P(("groups", "rep"), ("shard", "sub")),
    )
    cells = mesh.shape["shard"] * mesh.shape["sub"]
    reps = mesh.shape["rep"]

    def body(master, *rest):
        rows, columns = master.shape[1:]
        fits = reps == cells == 4 and rows % (4 * GROUP) == 0 and columns % (cells * 256) == 0
        if fits:
            return routed_body(cells, master, *rest)
        return general_body(master, *rest)

    return jax.shard_map(body, mesh=mesh, in_specs=in_specs, out_specs=out_specs, check_vma=False)
```

```python
import functools
import itertools

import jax
import jax.numpy as jnp
import numpy as np
from jax import lax
from jax.experimental import pallas as pl
from jax.experimental.pallas import tpu as pltpu
from jax.sharding import PartitionSpec as P

GROUP = 32
MOST = 2


LEVELS = 15.0
FLOOR = 0.02


def quantize(weights_block):
    row_count, col_count = weights_block.shape
    grouped = weights_block.reshape(row_count // GROUP, GROUP, col_count).astype(jnp.float32)
    lowest = jnp.min(grouped, axis=1)
    highest = jnp.max(grouped, axis=1)
    zero_point = lowest.astype(jnp.bfloat16)
    group_scale = (jnp.maximum(highest - lowest, FLOOR) / LEVELS).astype(jnp.bfloat16)
    code_values = (grouped - zero_point.astype(jnp.float32)[:, None, :]) / group_scale.astype(
        jnp.float32
    )[:, None, :]
    return (code_values.astype(jnp.bfloat16).reshape(row_count, col_count), group_scale, zero_point)


def restore(code_values, group_scale, zero_point):
    shape_full = code_values.shape
    grouped = code_values.reshape(
        shape_full[:-2] + (shape_full[-2] // GROUP, GROUP, shape_full[-1])
    ).astype(jnp.float32)
    restored = grouped * jnp.expand_dims(group_scale.astype(jnp.float32), -2) + jnp.expand_dims(
        zero_point.astype(jnp.float32), -2
    )
    return restored.astype(jnp.bfloat16).reshape(shape_full)


def local_slots(train_expert, rollout_owner, owner_index):
    total_experts = train_expert.shape[0]
    owners = rollout_owner[:, 0]
    labels = jnp.arange(total_experts, dtype=jnp.int32)
    same_owner = owners[:, None] == owners[None, :]
    ranking = jnp.sum((same_owner & (labels[None, :] < labels[:, None])).astype(jnp.int32), axis=1)
    own_mask = owners == owner_index
    chosen = []
    for slot_index in range(MOST):
        matched = own_mask & (ranking == slot_index)
        present = jnp.any(matched)
        expert_id = jnp.where(present, jnp.sum(jnp.where(matched, labels, 0)), -1)
        position = jnp.sum(jnp.where(train_expert == expert_id, labels, 0))
        chosen.append((expert_id, position, present))
    return chosen


def fold_select(chosen, selected, pieces, first_index):
    span = pieces[0].shape[0]
    result = []
    for member, held in zip(pieces, selected):
        layers = []
        for slot_index in range(MOST):
            expert_id, position, present = chosen[slot_index]
            inside = present & (position >= first_index) & (position < first_index + span)
            offset = jnp.clip(position, 0, span - 1)
            taken = lax.dynamic_index_in_dim(member, offset, 0, keepdims=False)
            layers.append(jnp.where(inside, taken, held[slot_index]))
        result.append(jnp.stack(layers))
    return tuple(result)


def general_body(master, train_expert, rollout_owner, hidden, routes, route_weight):
    local_rows = master[0]
    owner_index = lax.axis_index("rep")
    chosen = local_slots(train_expert, rollout_owner, owner_index)
    code_values, group_scale, zero_point = quantize(local_rows)
    relaid = (
        lax.all_to_all(code_values, ("shard", "sub"), split_axis=1, concat_axis=0, tiled=True),
        lax.all_to_all(group_scale, ("shard", "sub"), split_axis=1, concat_axis=0, tiled=True),
        lax.all_to_all(zero_point, ("shard", "sub"), split_axis=1, concat_axis=0, tiled=True),
    )
    start_slots = tuple((jnp.zeros((MOST,) + member.shape, member.dtype) for member in relaid))
    gathered = fold_select(
        chosen,
        start_slots,
        (
            lax.all_gather(relaid[0][None], "rep", axis=0, tiled=True),
            lax.all_gather(relaid[1][None], "rep", axis=0, tiled=True),
            lax.all_gather(relaid[2][None], "rep", axis=0, tiled=True),
        ),
        jnp.int32(0),
    )
    slot_codes = gathered[0]
    slot_values = restore(gathered[0], gathered[1], gathered[2])
    blended_list = []
    for slot_index in range(MOST):
        expert_id = chosen[slot_index][0]
        weight_here = jnp.where(routes == expert_id, route_weight, jnp.zeros((), jnp.float32))
        blended_list.append(jnp.sum(weight_here[:, :, None] * hidden, axis=1).astype(jnp.bfloat16))
    blended = jnp.stack(blended_list)
    all_blended = lax.all_gather(blended, ("shard", "sub"), axis=1, tiled=True)
    mixed = lax.psum_scatter(
        jnp.einsum("srf,sfd->rd", all_blended, slot_values, preferred_element_type=jnp.float32),
        "rep",
        scatter_dimension=0,
        tiled=True,
    ).astype(jnp.bfloat16)
    return (slot_codes[None], mixed)


CELL = ("shard", "sub")
VMEM_BYTES = 48 * 1024 * 1024
ROUNDS = 2
TILES = 2
LANES = 256
CODE_WEIGHT = 1


def moves(owners):
    return frozenset((p, owner) for p, owner in enumerate(owners) if owner != p)


def top_load(pairs, reps):
    return max(
        sum(low <= link < high for low, high in way)
        for way in ([(a, b) for a, b in pairs], [(b, a) for a, b in pairs])
        for link in range(reps - 1)
    )


def in_rounds(pairs):
    rounds = [[] for _ in range(ROUNDS)]

    def place(rest):
        if not rest:
            return True
        source, target = rest[0]
        for chosen in rounds:
            if all(source != a and target != b for a, b in chosen):
                chosen.append(rest[0])
                if place(rest[1:]):
                    return True
                chosen.pop()
        return False

    return rounds if place(sorted(pairs)) else None


@functools.lru_cache(maxsize=None)
def plans(reps):
    maps = [
        owners
        for owners in itertools.product(range(reps), repeat=reps)
        if max(owners.count(r) for r in range(reps)) <= MOST
    ]
    pairs = [(a, b) for a in range(reps) for b in range(reps) if a != b]
    chosen, table = [], np.zeros((reps**reps,), np.int32)
    for load in range(1, reps):
        todo = sorted(o for o in maps if max(1, top_load(moves(o), reps)) == load)
        if not todo:
            continue
        fitting = []
        for bits in range(1 << len(pairs)):
            subset = frozenset(pair for i, pair in enumerate(pairs) if bits >> i & 1)
            degrees = [sum(pair[side] == r for pair in subset) for side in (0, 1) for r in range(reps)]
            if max(degrees) <= ROUNDS and top_load(subset, reps) <= load:
                fitting.append(subset)
        while todo:
            best = max(fitting, key=lambda s: (sum(moves(o) <= s for o in todo), -len(s), sorted(s)))
            for owners in todo:
                if moves(owners) <= best:
                    table[sum(owner * reps**p for p, owner in enumerate(owners))] = len(chosen)
            todo = [o for o in todo if not moves(o) <= best]
            chosen.append(in_rounds(best))
    return chosen, table


def route_kernel(reps, train_ref, owner_ref, table_ref, round_ref, out_ref):
    rep = lax.axis_index("rep")
    cell = lax.axis_index(CELL)
    experts = [train_ref[p] for p in range(reps)]
    owners = [owner_ref[experts[p]] for p in range(reps)]
    number = sum(owners[p] * reps**p for p in range(reps))
    plan = table_ref[number]
    out_ref[0] = cell
    out_ref[1] = rep
    for slot in range(MOST):
        out_ref[2 + slot] = ROUNDS + 1
    for p in range(reps):
        rank = sum(
            ((owners[q] == owners[p]) & (experts[q] < experts[p])).astype(jnp.int32) for q in range(reps) if q != p
        )
        source = jnp.where(rep == p, 0, ROUNDS)
        for r in range(ROUNDS - 1):
            held = round_ref[(plan * ROUNDS + r) * reps + rep]
            source = jnp.where((rep != p) & (held == p), 1 + r, source)
        for slot in range(MOST):
            here = (owners[p] == rep) & (rank == slot)
            out_ref[2 + slot] = jnp.where(here, source, out_ref[2 + slot])
    out_ref[2 + MOST] = plan
    out_ref[3 + MOST] = train_ref[rep]


def route(train_expert, rollout_owner):
    reps = train_expert.shape[0]
    chosen, table = plans(reps)
    arrivals = np.full((len(chosen), ROUNDS, reps), -1, np.int32)
    for index, rounds in enumerate(chosen):
        for r, pairs in enumerate(rounds):
            for source, target in pairs:
                arrivals[index, r, target] = source
    smem = pl.BlockSpec(memory_space=pltpu.SMEM)
    return pl.pallas_call(
        functools.partial(route_kernel, reps),
        in_specs=[smem] * 4,
        out_specs=smem,
        out_shape=jax.ShapeDtypeStruct((4 + MOST,), jnp.int32),
        name="route",
    )(train_expert, rollout_owner[:, 0], jnp.asarray(table), jnp.asarray(arrivals.reshape(-1)))


SPAN = 8 * GROUP


def span_values(ref, first, lanes):
    rows = [pl.ds(first + g * GROUP, GROUP) for g in range(SPAN // GROUP)]
    lowest, highest = [], []
    for at in rows:
        block = ref[at, lanes]
        low = jnp.minimum(block[: GROUP // 2], block[GROUP // 2 :]).astype(jnp.float32)
        high = jnp.maximum(block[: GROUP // 2], block[GROUP // 2 :]).astype(jnp.float32)
        lowest.append(jnp.min(low, axis=0, keepdims=True))
        highest.append(jnp.max(high, axis=0, keepdims=True))
    lowest, highest = jnp.concatenate(lowest), jnp.concatenate(highest)
    scale = (jnp.maximum(highest - lowest, FLOOR) / LEVELS).astype(jnp.bfloat16).astype(jnp.float32)
    inverse = 1.0 / scale
    for g, at in enumerate(rows):
        zero = lowest[g : g + 1]
        codes = ((ref[at, lanes].astype(jnp.float32) - zero) * inverse[g : g + 1]).astype(jnp.bfloat16)
        yield g, codes, scale[g : g + 1], zero


def copy_kernel(scalars, *refs):
    count = 1 if len(refs) == 2 else 2
    for source_ref, out_ref in zip(refs[:count], refs[-count:]):
        out_ref[...] = source_ref[...]


def column_cost(rows, width):
    return pl.CostEstimate(flops=0, bytes_accessed=8 * rows * width, transcendentals=0)


def cut(scalars, master, cells):
    rows, width = master.shape[0], master.shape[1] // cells
    tile = rows // TILES
    return pl.pallas_call(
        copy_kernel,
        grid_spec=pltpu.PrefetchScalarGridSpec(
            num_scalar_prefetch=1,
            grid=(2, TILES),
            in_specs=[pl.BlockSpec((tile, width), lambda h, t, scalars: (t, scalars[0] ^ (1 + 2 * h)))],
            out_specs=[pl.BlockSpec((tile, width), lambda h, t, scalars: (h * TILES + t, 0))],
        ),
        out_shape=[jax.ShapeDtypeStruct((2 * rows, width), master.dtype)],
        compiler_params=pltpu.CompilerParams(vmem_limit_bytes=VMEM_BYTES),
        cost_estimate=column_cost(rows, width),
        name="cut",
    )(scalars, master)[0]


def join(scalars, master, other, cells):
    rows, width = master.shape[0], master.shape[1] // cells
    tile = rows // TILES
    shapes = [jax.ShapeDtypeStruct((2 * rows, width), master.dtype)] * 2
    own = pl.pallas_call(
        copy_kernel,
        grid_spec=pltpu.PrefetchScalarGridSpec(
            num_scalar_prefetch=1,
            grid=(TILES,),
            in_specs=[
                pl.BlockSpec((tile, width), lambda t, scalars: (t, scalars[0])),
                pl.BlockSpec((tile, width), lambda t, scalars: (t, scalars[0] ^ 2)),
            ],
            out_specs=[pl.BlockSpec((tile, width), lambda t, scalars: (t, 0))] * 2,
        ),
        out_shape=shapes,
        compiler_params=pltpu.CompilerParams(vmem_limit_bytes=VMEM_BYTES),
        cost_estimate=column_cost(rows, width),
        name="join_own",
    )(scalars, master, master)
    return pl.pallas_call(
        copy_kernel,
        grid_spec=pltpu.PrefetchScalarGridSpec(
            num_scalar_prefetch=1,
            grid=(TILES,),
            in_specs=[
                pl.BlockSpec((tile, width), lambda t, scalars: (t, 0)),
                pl.BlockSpec((tile, width), lambda t, scalars: (TILES + t, 0)),
                pl.BlockSpec(memory_space=pl.ANY),
                pl.BlockSpec(memory_space=pl.ANY),
            ],
            out_specs=[pl.BlockSpec((tile, width), lambda t, scalars: (TILES + t, 0))] * 2,
        ),
        out_shape=shapes,
        input_output_aliases={3: 0, 4: 1},
        compiler_params=pltpu.CompilerParams(vmem_limit_bytes=VMEM_BYTES),
        cost_estimate=column_cost(rows, width),
        name="join_other",
    )(scalars, other, other, *own)


def mix_kernel(cells, scalars, *refs):
    halves, blends = refs[:2], refs[2 : 2 + cells]
    away_ref, keep_ref, combined = refs[2 + cells :]
    me, rep = scalars[0], scalars[1]
    span, chunk = halves[0].shape[0] // 2, blends[0].shape[0]
    mate = rep ^ 1

    @pl.when(pl.program_id(0) == 0)
    def _():
        for step in range(cells):
            target = me ^ step
            place = jnp.where(target == mate, 0, jnp.where(target == 3 - mate, 1, jnp.where(target == rep, 2, 3)))
            combined[pl.ds(pl.multiple_of(place * chunk, 16), chunk), :] = blends[step][...]

    spans = span // SPAN
    total = jnp.zeros(combined.shape[:1] + away_ref.shape[1:], jnp.float32)
    for half in range(2):
        for n in range(2 * spans):
            first = (me ^ (2 * half + n // spans)) * span + n % spans * SPAN
            restored = [
                (codes.astype(jnp.float32) * scale + zero).astype(jnp.bfloat16)
                for g, codes, scale, zero in span_values(halves[half], n * SPAN, slice(None))
            ]
            total += jnp.dot(
                combined[:, pl.ds(pl.multiple_of(first, SPAN), SPAN)],
                jnp.concatenate(restored),
                preferred_element_type=jnp.float32,
            )
    away_ref[...] = total[: 2 * chunk].astype(away_ref.dtype)
    keep_ref[...] = total[2 * chunk :].astype(keep_ref.dtype)


def mix(scalars, halves, blends):
    cells = len(blends)
    rows, width = halves[0].shape
    chunk, depth = blends[0].shape
    tile = 256
    return pl.pallas_call(
        functools.partial(mix_kernel, cells),
        grid_spec=pltpu.PrefetchScalarGridSpec(
            num_scalar_prefetch=1,
            grid=(width // tile,),
            in_specs=[pl.BlockSpec((rows, tile), lambda i, scalars: (0, i))] * 2
            + [pl.BlockSpec((chunk, depth), lambda i, scalars: (0, 0))] * cells,
            out_specs=[pl.BlockSpec((2 * chunk, tile), lambda i, scalars: (0, i))] * 2,
            scratch_shapes=[
                pltpu.VMEM((cells * chunk, depth), jnp.bfloat16),
            ],
        ),
        out_shape=[jax.ShapeDtypeStruct((2 * chunk, width), jnp.bfloat16)] * 2,
        compiler_params=pltpu.CompilerParams(vmem_limit_bytes=VMEM_BYTES),
        cost_estimate=pl.CostEstimate(
            flops=2 * cells * chunk * depth * width,
            bytes_accessed=2 * (depth * width + cells * chunk * (depth + width)),
            transcendentals=0,
        ),
        name="mix",
    )(scalars, *halves, *blends)


def code_kernel(held, scalars, *refs):
    sources, out_ref, block = refs[:held], refs[-2], refs[-1]
    source = scalars[2 + pl.program_id(0)]
    for k in range(held):

        @pl.when(source == k)
        def _(k=k):
            block[...] = sources[k][...]

    @pl.when(source < held)
    def _():
        def piece(c, carry):
            lanes = pl.ds(pl.multiple_of(c * LANES, LANES), LANES)
            for first in range(0, out_ref.shape[2], SPAN):
                for g, codes, unused, unused in span_values(block, first, lanes):
                    out_ref[0, 0, first + g * GROUP : first + (g + 1) * GROUP, lanes] = codes
            return carry

        lax.fori_loop(0, out_ref.shape[3] // LANES, piece, 0)

    @pl.when(source == held)
    def _():
        out_ref[...] = jnp.zeros_like(out_ref)


def code(scalars, half, sources, so_far, depth):
    held = len(sources)
    rows, width = sources[0].shape
    tiles = 2 * TILES
    tile = rows // tiles

    def source_map(k):
        def index(slot, t, scalars):
            before = jnp.where((slot > 0) & (scalars[2] == k), tiles - 1, 0)
            return jnp.where(scalars[2 + slot] == k, t, before), 0

        return index

    def out_map(slot, t, scalars):
        return 0, slot, (scalars[0] ^ (2 * half + t // TILES)) * TILES + t % TILES, 0

    first = so_far is None
    return pl.pallas_call(
        functools.partial(code_kernel, held),
        grid_spec=pltpu.PrefetchScalarGridSpec(
            num_scalar_prefetch=1,
            grid=(MOST, tiles),
            in_specs=[pl.BlockSpec((tile, width), source_map(k)) for k in range(held)]
            + ([] if first else [pl.BlockSpec(memory_space=pl.ANY)]),
            out_specs=pl.BlockSpec((1, 1, tile, width), out_map),
            scratch_shapes=[pltpu.VMEM((tile, width), jnp.bfloat16)],
        ),
        out_shape=jax.ShapeDtypeStruct((1, MOST, depth, width), jnp.bfloat16),
        input_output_aliases={} if first else {1 + held: 0},
        compiler_params=pltpu.CompilerParams(vmem_limit_bytes=VMEM_BYTES),
        cost_estimate=pl.CostEstimate(
            flops=8 * MOST * rows * width, bytes_accessed=4 * MOST * rows * width * CODE_WEIGHT, transcendentals=0
        ),
        name=f"code_{half}",
    )(scalars, *sources, *([] if first else [so_far]))


def routed_body(cells, master, train_expert, rollout_owner, hidden, routes, route_weight):
    local_rows = master[0]
    reps = train_expert.shape[0]
    depth = cells * local_rows.shape[0]
    scalars = route(train_expert, rollout_owner)

    def swap(array, step):
        return lax.ppermute(array, CELL, [(c, c ^ step) for c in range(cells)])

    def planned(rounds):
        return lambda half: tuple(lax.ppermute(half, "rep", pairs) for pairs in rounds)

    def to_owners(half):
        return lax.switch(scalars[2 + MOST], [planned(rounds) for rounds in plans(reps)[0]], half)

    near, beyond = join(scalars, local_rows, swap(cut(scalars, local_rows, cells), 1), cells)
    far = swap(beyond, 2)
    weight_here = jnp.where(routes == scalars[3 + MOST], route_weight, jnp.zeros((), jnp.float32))
    blend = jnp.sum(weight_here[:, :, None] * hidden, axis=1).astype(jnp.bfloat16)
    beside, across = swap(blend, 1), swap(blend, 2)
    near_arrived = to_owners(near)
    far, across, beside, near_arrived = lax.optimization_barrier((far, across, beside, near_arrived))
    away, keep = mix(scalars, (near, far), [blend, beside, across, swap(across, 1)])
    far, away = lax.optimization_barrier((far, away))
    pair = keep.astype(jnp.float32) + lax.ppermute(away, "rep", [(r, r ^ 1) for r in range(reps)]).astype(jnp.float32)
    far_arrived = to_owners(far)
    pair, far_arrived = lax.optimization_barrier((pair, far_arrived))
    chunk = pair.shape[0] // 2
    rest = lax.ppermute(pair[chunk:].astype(jnp.bfloat16), "rep", [(r, reps - 1 - r) for r in range(reps)])
    mixed = (pair[:chunk] + rest.astype(jnp.float32)).astype(jnp.bfloat16)
    codes = code(scalars, 0, (near,) + near_arrived, None, depth)
    return code(scalars, 1, (far,) + far_arrived, codes, depth), mixed


def solution(mesh):
    in_specs = (
        P(("groups", "rep"), ("shard", "sub"), None),
        P(),
        P(),
        P(("groups", "shard", "sub"), None, None),
        P(("groups", "shard", "sub"), None),
        P(("groups", "shard", "sub"), None),
    )
    out_specs = (
        P(("groups", "rep"), None, None, ("shard", "sub")),
        P(("groups", "rep"), ("shard", "sub")),
    )
    cells = mesh.shape["shard"] * mesh.shape["sub"]
    reps = mesh.shape["rep"]

    def body(master, *rest):
        rows, columns = master.shape[1:]
        fits = reps == cells == 4 and rows % (4 * GROUP) == 0 and columns % (cells * 256) == 0
        if fits:
            return routed_body(cells, master, *rest)
        return general_body(master, *rest)

    return jax.shard_map(body, mesh=mesh, in_specs=in_specs, out_specs=out_specs, check_vma=False)
```

```python
import functools
import itertools

import jax
import jax.numpy as jnp
import numpy as np
from jax import lax
from jax.experimental import pallas as pl
from jax.experimental.pallas import tpu as pltpu
from jax.sharding import PartitionSpec as P

GROUP = 32
MOST = 2


LEVELS = 15.0
FLOOR = 0.02


def quantize(weights_block):
    row_count, col_count = weights_block.shape
    grouped = weights_block.reshape(row_count // GROUP, GROUP, col_count).astype(jnp.float32)
    lowest = jnp.min(grouped, axis=1)
    highest = jnp.max(grouped, axis=1)
    zero_point = lowest.astype(jnp.bfloat16)
    group_scale = (jnp.maximum(highest - lowest, FLOOR) / LEVELS).astype(jnp.bfloat16)
    code_values = (grouped - zero_point.astype(jnp.float32)[:, None, :]) / group_scale.astype(
        jnp.float32
    )[:, None, :]
    return (code_values.astype(jnp.bfloat16).reshape(row_count, col_count), group_scale, zero_point)


def restore(code_values, group_scale, zero_point):
    shape_full = code_values.shape
    grouped = code_values.reshape(
        shape_full[:-2] + (shape_full[-2] // GROUP, GROUP, shape_full[-1])
    ).astype(jnp.float32)
    restored = grouped * jnp.expand_dims(group_scale.astype(jnp.float32), -2) + jnp.expand_dims(
        zero_point.astype(jnp.float32), -2
    )
    return restored.astype(jnp.bfloat16).reshape(shape_full)


def local_slots(train_expert, rollout_owner, owner_index):
    total_experts = train_expert.shape[0]
    owners = rollout_owner[:, 0]
    labels = jnp.arange(total_experts, dtype=jnp.int32)
    same_owner = owners[:, None] == owners[None, :]
    ranking = jnp.sum((same_owner & (labels[None, :] < labels[:, None])).astype(jnp.int32), axis=1)
    own_mask = owners == owner_index
    chosen = []
    for slot_index in range(MOST):
        matched = own_mask & (ranking == slot_index)
        present = jnp.any(matched)
        expert_id = jnp.where(present, jnp.sum(jnp.where(matched, labels, 0)), -1)
        position = jnp.sum(jnp.where(train_expert == expert_id, labels, 0))
        chosen.append((expert_id, position, present))
    return chosen


def fold_select(chosen, selected, pieces, first_index):
    span = pieces[0].shape[0]
    result = []
    for member, held in zip(pieces, selected):
        layers = []
        for slot_index in range(MOST):
            expert_id, position, present = chosen[slot_index]
            inside = present & (position >= first_index) & (position < first_index + span)
            offset = jnp.clip(position, 0, span - 1)
            taken = lax.dynamic_index_in_dim(member, offset, 0, keepdims=False)
            layers.append(jnp.where(inside, taken, held[slot_index]))
        result.append(jnp.stack(layers))
    return tuple(result)


def general_body(master, train_expert, rollout_owner, hidden, routes, route_weight):
    local_rows = master[0]
    owner_index = lax.axis_index("rep")
    chosen = local_slots(train_expert, rollout_owner, owner_index)
    code_values, group_scale, zero_point = quantize(local_rows)
    relaid = (
        lax.all_to_all(code_values, ("shard", "sub"), split_axis=1, concat_axis=0, tiled=True),
        lax.all_to_all(group_scale, ("shard", "sub"), split_axis=1, concat_axis=0, tiled=True),
        lax.all_to_all(zero_point, ("shard", "sub"), split_axis=1, concat_axis=0, tiled=True),
    )
    start_slots = tuple((jnp.zeros((MOST,) + member.shape, member.dtype) for member in relaid))
    gathered = fold_select(
        chosen,
        start_slots,
        (
            lax.all_gather(relaid[0][None], "rep", axis=0, tiled=True),
            lax.all_gather(relaid[1][None], "rep", axis=0, tiled=True),
            lax.all_gather(relaid[2][None], "rep", axis=0, tiled=True),
        ),
        jnp.int32(0),
    )
    slot_codes = gathered[0]
    slot_values = restore(gathered[0], gathered[1], gathered[2])
    blended_list = []
    for slot_index in range(MOST):
        expert_id = chosen[slot_index][0]
        weight_here = jnp.where(routes == expert_id, route_weight, jnp.zeros((), jnp.float32))
        blended_list.append(jnp.sum(weight_here[:, :, None] * hidden, axis=1).astype(jnp.bfloat16))
    blended = jnp.stack(blended_list)
    all_blended = lax.all_gather(blended, ("shard", "sub"), axis=1, tiled=True)
    mixed = lax.psum_scatter(
        jnp.einsum("srf,sfd->rd", all_blended, slot_values, preferred_element_type=jnp.float32),
        "rep",
        scatter_dimension=0,
        tiled=True,
    ).astype(jnp.bfloat16)
    return (slot_codes[None], mixed)


CELL = ("shard", "sub")
VMEM_BYTES = 32 * 1024 * 1024
SMALL_BYTES = 16 * 1024 * 1024
ROUNDS = 2
TILES = 2
LANES = 256
CODE_WEIGHT = 1


def moves(owners):
    return frozenset((p, owner) for p, owner in enumerate(owners) if owner != p)


def top_load(pairs, reps):
    return max(
        sum(low <= link < high for low, high in way)
        for way in ([(a, b) for a, b in pairs], [(b, a) for a, b in pairs])
        for link in range(reps - 1)
    )


def in_rounds(pairs):
    rounds = [[] for _ in range(ROUNDS)]

    def place(rest):
        if not rest:
            return True
        source, target = rest[0]
        for chosen in rounds:
            if all(source != a and target != b for a, b in chosen):
                chosen.append(rest[0])
                if place(rest[1:]):
                    return True
                chosen.pop()
        return False

    return rounds if place(sorted(pairs)) else None


@functools.lru_cache(maxsize=None)
def plans(reps):
    maps = [
        owners
        for owners in itertools.product(range(reps), repeat=reps)
        if max(owners.count(r) for r in range(reps)) <= MOST
    ]
    pairs = [(a, b) for a in range(reps) for b in range(reps) if a != b]
    chosen, table = [], np.zeros((reps**reps,), np.int32)
    for load in range(1, reps):
        todo = sorted(o for o in maps if max(1, top_load(moves(o), reps)) == load)
        if not todo:
            continue
        fitting = []
        for bits in range(1 << len(pairs)):
            subset = frozenset(pair for i, pair in enumerate(pairs) if bits >> i & 1)
            degrees = [sum(pair[side] == r for pair in subset) for side in (0, 1) for r in range(reps)]
            if max(degrees) <= ROUNDS and top_load(subset, reps) <= load:
                fitting.append(subset)
        while todo:
            best = max(fitting, key=lambda s: (sum(moves(o) <= s for o in todo), -len(s), sorted(s)))
            for owners in todo:
                if moves(owners) <= best:
                    table[sum(owner * reps**p for p, owner in enumerate(owners))] = len(chosen)
            todo = [o for o in todo if not moves(o) <= best]
            chosen.append(in_rounds(best))
    return chosen, table


def route_kernel(reps, train_ref, owner_ref, table_ref, round_ref, out_ref):
    rep = lax.axis_index("rep")
    cell = lax.axis_index(CELL)
    experts = [train_ref[p] for p in range(reps)]
    owners = [owner_ref[experts[p]] for p in range(reps)]
    number = sum(owners[p] * reps**p for p in range(reps))
    plan = table_ref[number]
    out_ref[0] = cell
    out_ref[1] = rep
    for slot in range(MOST):
        out_ref[2 + slot] = ROUNDS + 1
    for p in range(reps):
        rank = sum(
            ((owners[q] == owners[p]) & (experts[q] < experts[p])).astype(jnp.int32) for q in range(reps) if q != p
        )
        source = jnp.where(rep == p, 0, ROUNDS)
        for r in range(ROUNDS - 1):
            held = round_ref[(plan * ROUNDS + r) * reps + rep]
            source = jnp.where((rep != p) & (held == p), 1 + r, source)
        for slot in range(MOST):
            here = (owners[p] == rep) & (rank == slot)
            out_ref[2 + slot] = jnp.where(here, source, out_ref[2 + slot])
    out_ref[2 + MOST] = plan
    out_ref[3 + MOST] = train_ref[rep]


def route(train_expert, rollout_owner):
    reps = train_expert.shape[0]
    chosen, table = plans(reps)
    arrivals = np.full((len(chosen), ROUNDS, reps), -1, np.int32)
    for index, rounds in enumerate(chosen):
        for r, pairs in enumerate(rounds):
            for source, target in pairs:
                arrivals[index, r, target] = source
    smem = pl.BlockSpec(memory_space=pltpu.SMEM)
    return pl.pallas_call(
        functools.partial(route_kernel, reps),
        in_specs=[smem] * 4,
        out_specs=smem,
        out_shape=jax.ShapeDtypeStruct((4 + MOST,), jnp.int32),
        name="route",
    )(train_expert, rollout_owner[:, 0], jnp.asarray(table), jnp.asarray(arrivals.reshape(-1)))


SPAN = 8 * GROUP


def span_values(ref, first, lanes):
    rows = [pl.ds(first + g * GROUP, GROUP) for g in range(SPAN // GROUP)]
    lowest, highest = [], []
    for at in rows:
        block = ref[at, lanes]
        low = jnp.minimum(block[: GROUP // 2], block[GROUP // 2 :]).astype(jnp.float32)
        high = jnp.maximum(block[: GROUP // 2], block[GROUP // 2 :]).astype(jnp.float32)
        lowest.append(jnp.min(low, axis=0, keepdims=True))
        highest.append(jnp.max(high, axis=0, keepdims=True))
    lowest, highest = jnp.concatenate(lowest), jnp.concatenate(highest)
    scale = (jnp.maximum(highest - lowest, FLOOR) / LEVELS).astype(jnp.bfloat16).astype(jnp.float32)
    inverse = 1.0 / scale
    for g, at in enumerate(rows):
        zero = lowest[g : g + 1]
        codes = ((ref[at, lanes].astype(jnp.float32) - zero) * inverse[g : g + 1]).astype(jnp.bfloat16)
        yield g, codes, scale[g : g + 1], zero


def copy_kernel(scalars, *refs):
    count = 1 if len(refs) == 2 else 2
    for source_ref, out_ref in zip(refs[:count], refs[-count:]):
        out_ref[...] = source_ref[...]


def column_cost(rows, width):
    return pl.CostEstimate(flops=0, bytes_accessed=8 * rows * width, transcendentals=0)


def cut(scalars, master, cells):
    rows, width = master.shape[0], master.shape[1] // cells
    tile = rows // TILES
    return pl.pallas_call(
        copy_kernel,
        grid_spec=pltpu.PrefetchScalarGridSpec(
            num_scalar_prefetch=1,
            grid=(2, TILES),
            in_specs=[pl.BlockSpec((tile, width), lambda h, t, scalars: (t, scalars[0] ^ (1 + 2 * h)))],
            out_specs=[pl.BlockSpec((tile, width), lambda h, t, scalars: (h * TILES + t, 0))],
        ),
        out_shape=[jax.ShapeDtypeStruct((2 * rows, width), master.dtype)],
        compiler_params=pltpu.CompilerParams(vmem_limit_bytes=SMALL_BYTES),
        cost_estimate=column_cost(rows, width),
        name="cut",
    )(scalars, master)[0]


def join(scalars, master, other, cells):
    rows, width = master.shape[0], master.shape[1] // cells
    tile = rows // TILES
    shapes = [jax.ShapeDtypeStruct((2 * rows, width), master.dtype)] * 2
    own = pl.pallas_call(
        copy_kernel,
        grid_spec=pltpu.PrefetchScalarGridSpec(
            num_scalar_prefetch=1,
            grid=(TILES,),
            in_specs=[
                pl.BlockSpec((tile, width), lambda t, scalars: (t, scalars[0])),
                pl.BlockSpec((tile, width), lambda t, scalars: (t, scalars[0] ^ 2)),
            ],
            out_specs=[pl.BlockSpec((tile, width), lambda t, scalars: (t, 0))] * 2,
        ),
        out_shape=shapes,
        compiler_params=pltpu.CompilerParams(vmem_limit_bytes=SMALL_BYTES),
        cost_estimate=column_cost(rows, width),
        name="join_own",
    )(scalars, master, master)
    return pl.pallas_call(
        copy_kernel,
        grid_spec=pltpu.PrefetchScalarGridSpec(
            num_scalar_prefetch=1,
            grid=(TILES,),
            in_specs=[
                pl.BlockSpec((tile, width), lambda t, scalars: (t, 0)),
                pl.BlockSpec((tile, width), lambda t, scalars: (TILES + t, 0)),
                pl.BlockSpec(memory_space=pl.ANY),
                pl.BlockSpec(memory_space=pl.ANY),
            ],
            out_specs=[pl.BlockSpec((tile, width), lambda t, scalars: (TILES + t, 0))] * 2,
        ),
        out_shape=shapes,
        input_output_aliases={3: 0, 4: 1},
        compiler_params=pltpu.CompilerParams(vmem_limit_bytes=SMALL_BYTES),
        cost_estimate=column_cost(rows, width),
        name="join_other",
    )(scalars, other, other, *own)


def blend_kernel(scalars, hidden_ref, routes_ref, weights_ref, out_ref):
    weights = jnp.where(routes_ref[...] == scalars[3 + MOST], weights_ref[...], 0.0).T
    hidden = hidden_ref[...].astype(jnp.float32)
    total = weights[:, 0:1] * hidden[:, 0, :]
    for k in range(1, hidden.shape[1]):
        total += weights[:, k : k + 1] * hidden[:, k, :]
    out_ref[...] = total.astype(out_ref.dtype)


def blend_rows(scalars, hidden, routes, route_weight):
    rows, top, depth = hidden.shape
    tile = depth // TILES
    table = pl.BlockSpec((top, rows), lambda i, scalars: (0, 0))
    return pl.pallas_call(
        blend_kernel,
        grid_spec=pltpu.PrefetchScalarGridSpec(
            num_scalar_prefetch=1,
            grid=(TILES,),
            in_specs=[pl.BlockSpec((rows, top, tile), lambda i, scalars: (0, 0, i)), table, table],
            out_specs=pl.BlockSpec((rows, tile), lambda i, scalars: (0, i)),
        ),
        out_shape=jax.ShapeDtypeStruct((rows, depth), jnp.bfloat16),
        cost_estimate=pl.CostEstimate(flops=0, bytes_accessed=6 * rows * depth, transcendentals=0),
        name="blend",
    )(scalars, hidden, routes.T, route_weight.T)


def mix_kernel(cells, scalars, *refs):
    halves, blends = refs[:2], refs[2 : 2 + cells]
    away_ref, keep_ref, combined = refs[2 + cells :]
    me, rep = scalars[0], scalars[1]
    span, chunk = halves[0].shape[0] // 2, blends[0].shape[0]
    mate = rep ^ 1

    @pl.when(pl.program_id(0) == 0)
    def _():
        for step in range(cells):
            target = me ^ step
            place = jnp.where(target == mate, 0, jnp.where(target == 3 - mate, 1, jnp.where(target == rep, 2, 3)))
            combined[pl.ds(pl.multiple_of(place * chunk, 16), chunk), :] = blends[step][...]

    spans = span // SPAN
    total = jnp.zeros(combined.shape[:1] + away_ref.shape[1:], jnp.float32)
    for half in range(2):
        for n in range(2 * spans):
            first = (me ^ (2 * half + n // spans)) * span + n % spans * SPAN
            restored = [
                (codes.astype(jnp.float32) * scale + zero).astype(jnp.bfloat16)
                for g, codes, scale, zero in span_values(halves[half], n * SPAN, slice(None))
            ]
            total += jnp.dot(
                combined[:, pl.ds(pl.multiple_of(first, SPAN), SPAN)],
                jnp.concatenate(restored),
                preferred_element_type=jnp.float32,
            )
    away_ref[...] = total[: 2 * chunk].astype(away_ref.dtype)
    keep_ref[...] = total[2 * chunk :].astype(keep_ref.dtype)


def mix(scalars, halves, blends):
    cells = len(blends)
    rows, width = halves[0].shape
    chunk, depth = blends[0].shape
    tile = 256
    return pl.pallas_call(
        functools.partial(mix_kernel, cells),
        grid_spec=pltpu.PrefetchScalarGridSpec(
            num_scalar_prefetch=1,
            grid=(width // tile,),
            in_specs=[pl.BlockSpec((rows, tile), lambda i, scalars: (0, i))] * 2
            + [pl.BlockSpec((chunk, depth), lambda i, scalars: (0, 0))] * cells,
            out_specs=[pl.BlockSpec((2 * chunk, tile), lambda i, scalars: (0, i))] * 2,
            scratch_shapes=[
                pltpu.VMEM((cells * chunk, depth), jnp.bfloat16),
            ],
        ),
        out_shape=[jax.ShapeDtypeStruct((2 * chunk, width), jnp.bfloat16)] * 2,
        compiler_params=pltpu.CompilerParams(vmem_limit_bytes=VMEM_BYTES),
        cost_estimate=pl.CostEstimate(
            flops=2 * cells * chunk * depth * width,
            bytes_accessed=2 * (depth * width + cells * chunk * (depth + width)),
            transcendentals=0,
        ),
        name="mix",
    )(scalars, *halves, *blends)


def code_kernel(held, scalars, *refs):
    sources, out_ref, block = refs[:held], refs[-2], refs[-1]
    source = scalars[2 + pl.program_id(0)]
    for k in range(held):

        @pl.when(source == k)
        def _(k=k):
            block[...] = sources[k][...]

    @pl.when(source < held)
    def _():
        def piece(c, carry):
            lanes = pl.ds(pl.multiple_of(c * LANES, LANES), LANES)
            for first in range(0, out_ref.shape[2], SPAN):
                for g, codes, unused, unused in span_values(block, first, lanes):
                    out_ref[0, 0, first + g * GROUP : first + (g + 1) * GROUP, lanes] = codes
            return carry

        lax.fori_loop(0, out_ref.shape[3] // LANES, piece, 0)

    @pl.when(source == held)
    def _():
        out_ref[...] = jnp.zeros_like(out_ref)


def code(scalars, half, sources, so_far, depth):
    held = len(sources)
    rows, width = sources[0].shape
    tiles = 2 * TILES
    tile = rows // tiles

    def source_map(k):
        def index(slot, t, scalars):
            before = jnp.where((slot > 0) & (scalars[2] == k), tiles - 1, 0)
            return jnp.where(scalars[2 + slot] == k, t, before), 0

        return index

    def out_map(slot, t, scalars):
        return 0, slot, (scalars[0] ^ (2 * half + t // TILES)) * TILES + t % TILES, 0

    first = so_far is None
    return pl.pallas_call(
        functools.partial(code_kernel, held),
        grid_spec=pltpu.PrefetchScalarGridSpec(
            num_scalar_prefetch=1,
            grid=(MOST, tiles),
            in_specs=[pl.BlockSpec((tile, width), source_map(k)) for k in range(held)]
            + ([] if first else [pl.BlockSpec(memory_space=pl.ANY)]),
            out_specs=pl.BlockSpec((1, 1, tile, width), out_map),
            scratch_shapes=[pltpu.VMEM((tile, width), jnp.bfloat16)],
        ),
        out_shape=jax.ShapeDtypeStruct((1, MOST, depth, width), jnp.bfloat16),
        input_output_aliases={} if first else {1 + held: 0},
        compiler_params=pltpu.CompilerParams(vmem_limit_bytes=SMALL_BYTES),
        cost_estimate=pl.CostEstimate(
            flops=8 * MOST * rows * width, bytes_accessed=4 * MOST * rows * width * CODE_WEIGHT, transcendentals=0
        ),
        name=f"code_{half}",
    )(scalars, *sources, *([] if first else [so_far]))


def routed_body(cells, master, train_expert, rollout_owner, hidden, routes, route_weight):
    local_rows = master[0]
    reps = train_expert.shape[0]
    depth = cells * local_rows.shape[0]
    scalars = route(train_expert, rollout_owner)

    def swap(array, step):
        return lax.ppermute(array, CELL, [(c, c ^ step) for c in range(cells)])

    def to_owners(branch, *operands):
        return lax.switch(scalars[2 + MOST], [branch(rounds) for rounds in plans(reps)[0]], *operands)

    def moved(rounds, half):
        return tuple(lax.ppermute(half, "rep", pairs) for pairs in rounds)

    def near_moves(rounds):
        return lambda near, beyond, blend: (moved(rounds, near), swap(beyond, 2), swap(blend, 1))

    def far_moves(rounds):
        return lambda away, far: (lax.ppermute(away, "rep", [(r, r ^ 1) for r in range(reps)]), moved(rounds, far))

    blend = blend_rows(scalars, hidden, routes, route_weight)
    across = swap(blend, 2)
    local_rows, blend = lax.optimization_barrier((local_rows, blend))
    near, beyond = join(scalars, local_rows, swap(cut(scalars, local_rows, cells), 1), cells)
    near_arrived, far, beside = to_owners(near_moves, near, beyond, blend)
    across, far = lax.optimization_barrier((across, far))
    away, keep = mix(scalars, (near, far), [blend, beside, across, swap(across, 1)])
    brought, far_arrived = to_owners(far_moves, away, far)
    chunk = keep.shape[0] // 2

    def added(part, *terms):
        return sum(term[part].astype(jnp.float32) for term in terms)

    rest = lax.ppermute(
        added(slice(chunk, None), keep, brought).astype(jnp.bfloat16), "rep", [(r, reps - 1 - r) for r in range(reps)]
    )
    keep, brought, rest = lax.optimization_barrier((keep, brought, rest))
    mixed = added(slice(chunk), keep, brought, rest).astype(jnp.bfloat16)
    codes = code(scalars, 0, (near,) + near_arrived, None, depth)
    return code(scalars, 1, (far,) + far_arrived, codes, depth), mixed


def solution(mesh):
    in_specs = (
        P(("groups", "rep"), ("shard", "sub"), None),
        P(),
        P(),
        P(("groups", "shard", "sub"), None, None),
        P(("groups", "shard", "sub"), None),
        P(("groups", "shard", "sub"), None),
    )
    out_specs = (
        P(("groups", "rep"), None, None, ("shard", "sub")),
        P(("groups", "rep"), ("shard", "sub")),
    )
    cells = mesh.shape["shard"] * mesh.shape["sub"]
    reps = mesh.shape["rep"]

    def body(master, *rest):
        rows, columns = master.shape[1:]
        fits = reps == cells == 4 and rows % (4 * GROUP) == 0 and columns % (cells * 256) == 0
        if fits:
            return routed_body(cells, master, *rest)
        return general_body(master, *rest)

    return jax.shard_map(body, mesh=mesh, in_specs=in_specs, out_specs=out_specs, check_vma=False)
```

```python
import functools
import itertools

import jax
import jax.numpy as jnp
import numpy as np
from jax import lax
from jax.experimental import pallas as pl
from jax.experimental.pallas import tpu as pltpu
from jax.sharding import PartitionSpec as P

GROUP = 32
MOST = 2


LEVELS = 15.0
FLOOR = 0.02


def quantize(weights_block):
    row_count, col_count = weights_block.shape
    grouped = weights_block.reshape(row_count // GROUP, GROUP, col_count).astype(jnp.float32)
    lowest = jnp.min(grouped, axis=1)
    highest = jnp.max(grouped, axis=1)
    zero_point = lowest.astype(jnp.bfloat16)
    group_scale = (jnp.maximum(highest - lowest, FLOOR) / LEVELS).astype(jnp.bfloat16)
    code_values = (grouped - zero_point.astype(jnp.float32)[:, None, :]) / group_scale.astype(
        jnp.float32
    )[:, None, :]
    return (code_values.astype(jnp.bfloat16).reshape(row_count, col_count), group_scale, zero_point)


def restore(code_values, group_scale, zero_point):
    shape_full = code_values.shape
    grouped = code_values.reshape(
        shape_full[:-2] + (shape_full[-2] // GROUP, GROUP, shape_full[-1])
    ).astype(jnp.float32)
    restored = grouped * jnp.expand_dims(group_scale.astype(jnp.float32), -2) + jnp.expand_dims(
        zero_point.astype(jnp.float32), -2
    )
    return restored.astype(jnp.bfloat16).reshape(shape_full)


def local_slots(train_expert, rollout_owner, owner_index):
    total_experts = train_expert.shape[0]
    owners = rollout_owner[:, 0]
    labels = jnp.arange(total_experts, dtype=jnp.int32)
    same_owner = owners[:, None] == owners[None, :]
    ranking = jnp.sum((same_owner & (labels[None, :] < labels[:, None])).astype(jnp.int32), axis=1)
    own_mask = owners == owner_index
    chosen = []
    for slot_index in range(MOST):
        matched = own_mask & (ranking == slot_index)
        present = jnp.any(matched)
        expert_id = jnp.where(present, jnp.sum(jnp.where(matched, labels, 0)), -1)
        position = jnp.sum(jnp.where(train_expert == expert_id, labels, 0))
        chosen.append((expert_id, position, present))
    return chosen


def fold_select(chosen, selected, pieces, first_index):
    span = pieces[0].shape[0]
    result = []
    for member, held in zip(pieces, selected):
        layers = []
        for slot_index in range(MOST):
            expert_id, position, present = chosen[slot_index]
            inside = present & (position >= first_index) & (position < first_index + span)
            offset = jnp.clip(position, 0, span - 1)
            taken = lax.dynamic_index_in_dim(member, offset, 0, keepdims=False)
            layers.append(jnp.where(inside, taken, held[slot_index]))
        result.append(jnp.stack(layers))
    return tuple(result)


def general_body(master, train_expert, rollout_owner, hidden, routes, route_weight):
    local_rows = master[0]
    owner_index = lax.axis_index("rep")
    chosen = local_slots(train_expert, rollout_owner, owner_index)
    code_values, group_scale, zero_point = quantize(local_rows)
    relaid = (
        lax.all_to_all(code_values, ("shard", "sub"), split_axis=1, concat_axis=0, tiled=True),
        lax.all_to_all(group_scale, ("shard", "sub"), split_axis=1, concat_axis=0, tiled=True),
        lax.all_to_all(zero_point, ("shard", "sub"), split_axis=1, concat_axis=0, tiled=True),
    )
    start_slots = tuple((jnp.zeros((MOST,) + member.shape, member.dtype) for member in relaid))
    gathered = fold_select(
        chosen,
        start_slots,
        (
            lax.all_gather(relaid[0][None], "rep", axis=0, tiled=True),
            lax.all_gather(relaid[1][None], "rep", axis=0, tiled=True),
            lax.all_gather(relaid[2][None], "rep", axis=0, tiled=True),
        ),
        jnp.int32(0),
    )
    slot_codes = gathered[0]
    slot_values = restore(gathered[0], gathered[1], gathered[2])
    blended_list = []
    for slot_index in range(MOST):
        expert_id = chosen[slot_index][0]
        weight_here = jnp.where(routes == expert_id, route_weight, jnp.zeros((), jnp.float32))
        blended_list.append(jnp.sum(weight_here[:, :, None] * hidden, axis=1).astype(jnp.bfloat16))
    blended = jnp.stack(blended_list)
    all_blended = lax.all_gather(blended, ("shard", "sub"), axis=1, tiled=True)
    mixed = lax.psum_scatter(
        jnp.einsum("srf,sfd->rd", all_blended, slot_values, preferred_element_type=jnp.float32),
        "rep",
        scatter_dimension=0,
        tiled=True,
    ).astype(jnp.bfloat16)
    return (slot_codes[None], mixed)


CELL = ("shard", "sub")
VMEM_BYTES = 32 * 1024 * 1024
SMALL_BYTES = 16 * 1024 * 1024
ROUNDS = 2
TILES = 2
LANES = 256
CODE_WEIGHT = 1


def moves(owners):
    return frozenset((p, owner) for p, owner in enumerate(owners) if owner != p)


def top_loads(pairs, reps):
    loads = [
        [sum(low <= link < high for low, high in way) for link in range(reps - 1)]
        for way in ([(a, b) for a, b in pairs], [(b, a) for a, b in pairs])
    ]
    return max(map(max, loads)), max(max(load[::2]) for load in loads)


def in_rounds(pairs):
    rounds = [[] for _ in range(ROUNDS)]

    def place(rest):
        if not rest:
            return True
        source, target = rest[0]
        for chosen in rounds:
            if all(source != a and target != b for a, b in chosen):
                chosen.append(rest[0])
                if place(rest[1:]):
                    return True
                chosen.pop()
        return False

    return rounds if place(sorted(pairs)) else None


@functools.lru_cache(maxsize=None)
def plans(reps):
    maps = [
        owners
        for owners in itertools.product(range(reps), repeat=reps)
        if max(owners.count(r) for r in range(reps)) <= MOST
    ]
    pairs = [(a, b) for a in range(reps) for b in range(reps) if a != b]
    chosen, table = [], np.zeros((reps**reps,), np.int32)
    kinds = {owners: top_loads(moves(owners), reps) for owners in maps}
    for kind in sorted(set(kinds.values())):
        todo = sorted(owners for owners in maps if kinds[owners] == kind)
        fitting = []
        for bits in range(1 << len(pairs)):
            subset = frozenset(pair for i, pair in enumerate(pairs) if bits >> i & 1)
            degrees = [sum(pair[side] == r for pair in subset) for side in (0, 1) for r in range(reps)]
            if max(degrees) <= ROUNDS and all(x <= y for x, y in zip(top_loads(subset, reps), kind)):
                fitting.append(subset)
        while todo:
            best = max(fitting, key=lambda s: (sum(moves(o) <= s for o in todo), -len(s), sorted(s)))
            for owners in todo:
                if moves(owners) <= best:
                    table[sum(owner * reps**p for p, owner in enumerate(owners))] = len(chosen)
            todo = [o for o in todo if not moves(o) <= best]
            chosen.append(in_rounds(best))
    return chosen, table


def route_kernel(reps, train_ref, owner_ref, table_ref, round_ref, out_ref):
    rep = lax.axis_index("rep")
    cell = lax.axis_index(CELL)
    experts = [train_ref[p] for p in range(reps)]
    owners = [owner_ref[experts[p]] for p in range(reps)]
    number = sum(owners[p] * reps**p for p in range(reps))
    plan = table_ref[number]
    out_ref[0] = cell
    out_ref[1] = rep
    for slot in range(MOST):
        out_ref[2 + slot] = ROUNDS + 1
    for p in range(reps):
        rank = sum(
            ((owners[q] == owners[p]) & (experts[q] < experts[p])).astype(jnp.int32) for q in range(reps) if q != p
        )
        source = jnp.where(rep == p, 0, ROUNDS)
        for r in range(ROUNDS - 1):
            held = round_ref[(plan * ROUNDS + r) * reps + rep]
            source = jnp.where((rep != p) & (held == p), 1 + r, source)
        for slot in range(MOST):
            here = (owners[p] == rep) & (rank == slot)
            out_ref[2 + slot] = jnp.where(here, source, out_ref[2 + slot])
    out_ref[2 + MOST] = plan
    out_ref[3 + MOST] = train_ref[rep]


def route(train_expert, rollout_owner):
    reps = train_expert.shape[0]
    chosen, table = plans(reps)
    arrivals = np.full((len(chosen), ROUNDS, reps), -1, np.int32)
    for index, rounds in enumerate(chosen):
        for r, pairs in enumerate(rounds):
            for source, target in pairs:
                arrivals[index, r, target] = source
    smem = pl.BlockSpec(memory_space=pltpu.SMEM)
    return pl.pallas_call(
        functools.partial(route_kernel, reps),
        in_specs=[smem] * 4,
        out_specs=smem,
        out_shape=jax.ShapeDtypeStruct((4 + MOST,), jnp.int32),
        name="route",
    )(train_expert, rollout_owner[:, 0], jnp.asarray(table), jnp.asarray(arrivals.reshape(-1)))


SPAN = 8 * GROUP


def span_values(ref, first, lanes):
    rows = [pl.ds(first + g * GROUP, GROUP) for g in range(SPAN // GROUP)]
    lowest, highest = [], []
    for at in rows:
        block = ref[at, lanes]
        low = jnp.minimum(block[: GROUP // 2], block[GROUP // 2 :]).astype(jnp.float32)
        high = jnp.maximum(block[: GROUP // 2], block[GROUP // 2 :]).astype(jnp.float32)
        lowest.append(jnp.min(low, axis=0, keepdims=True))
        highest.append(jnp.max(high, axis=0, keepdims=True))
    lowest, highest = jnp.concatenate(lowest), jnp.concatenate(highest)
    scale = (jnp.maximum(highest - lowest, FLOOR) / LEVELS).astype(jnp.bfloat16).astype(jnp.float32)
    inverse = 1.0 / scale
    for g, at in enumerate(rows):
        zero = lowest[g : g + 1]
        codes = ((ref[at, lanes].astype(jnp.float32) - zero) * inverse[g : g + 1]).astype(jnp.bfloat16)
        yield g, codes, scale[g : g + 1], zero


def copy_kernel(scalars, *refs):
    count = 1 if len(refs) == 2 else 2
    for source_ref, out_ref in zip(refs[:count], refs[-count:]):
        out_ref[...] = source_ref[...]


def column_cost(rows, width):
    return pl.CostEstimate(flops=0, bytes_accessed=8 * rows * width, transcendentals=0)


def cut(scalars, master, cells):
    rows, width = master.shape[0], master.shape[1] // cells
    tile = rows // TILES
    return pl.pallas_call(
        copy_kernel,
        grid_spec=pltpu.PrefetchScalarGridSpec(
            num_scalar_prefetch=1,
            grid=(2, TILES),
            in_specs=[pl.BlockSpec((tile, width), lambda h, t, scalars: (t, scalars[0] ^ (1 + 2 * h)))],
            out_specs=[pl.BlockSpec((tile, width), lambda h, t, scalars: (h * TILES + t, 0))],
        ),
        out_shape=[jax.ShapeDtypeStruct((2 * rows, width), master.dtype)],
        compiler_params=pltpu.CompilerParams(vmem_limit_bytes=SMALL_BYTES),
        cost_estimate=column_cost(rows, width),
        name="cut",
    )(scalars, master)[0]


def join(scalars, master, other, cells):
    rows, width = master.shape[0], master.shape[1] // cells
    tile = rows // TILES
    shapes = [jax.ShapeDtypeStruct((2 * rows, width), master.dtype)] * 2
    own = pl.pallas_call(
        copy_kernel,
        grid_spec=pltpu.PrefetchScalarGridSpec(
            num_scalar_prefetch=1,
            grid=(TILES,),
            in_specs=[
                pl.BlockSpec((tile, width), lambda t, scalars: (t, scalars[0])),
                pl.BlockSpec((tile, width), lambda t, scalars: (t, scalars[0] ^ 2)),
            ],
            out_specs=[pl.BlockSpec((tile, width), lambda t, scalars: (t, 0))] * 2,
        ),
        out_shape=shapes,
        compiler_params=pltpu.CompilerParams(vmem_limit_bytes=SMALL_BYTES),
        cost_estimate=column_cost(rows, width),
        name="join_own",
    )(scalars, master, master)
    return pl.pallas_call(
        copy_kernel,
        grid_spec=pltpu.PrefetchScalarGridSpec(
            num_scalar_prefetch=1,
            grid=(TILES,),
            in_specs=[
                pl.BlockSpec((tile, width), lambda t, scalars: (t, 0)),
                pl.BlockSpec((tile, width), lambda t, scalars: (TILES + t, 0)),
                pl.BlockSpec(memory_space=pl.ANY),
                pl.BlockSpec(memory_space=pl.ANY),
            ],
            out_specs=[pl.BlockSpec((tile, width), lambda t, scalars: (TILES + t, 0))] * 2,
        ),
        out_shape=shapes,
        input_output_aliases={3: 0, 4: 1},
        compiler_params=pltpu.CompilerParams(vmem_limit_bytes=SMALL_BYTES),
        cost_estimate=column_cost(rows, width),
        name="join_other",
    )(scalars, other, other, *own)


def blend_kernel(scalars, hidden_ref, routes_ref, weights_ref, out_ref):
    weights = jnp.where(routes_ref[...] == scalars[3 + MOST], weights_ref[...], 0.0).T
    hidden = hidden_ref[...].astype(jnp.float32)
    total = weights[:, 0:1] * hidden[:, 0, :]
    for k in range(1, hidden.shape[1]):
        total += weights[:, k : k + 1] * hidden[:, k, :]
    out_ref[...] = total.astype(out_ref.dtype)


def blend_rows(scalars, hidden, routes, route_weight):
    rows, top, depth = hidden.shape
    tile = depth // TILES
    table = pl.BlockSpec((top, rows), lambda i, scalars: (0, 0))
    return pl.pallas_call(
        blend_kernel,
        grid_spec=pltpu.PrefetchScalarGridSpec(
            num_scalar_prefetch=1,
            grid=(TILES,),
            in_specs=[pl.BlockSpec((rows, top, tile), lambda i, scalars: (0, 0, i)), table, table],
            out_specs=pl.BlockSpec((rows, tile), lambda i, scalars: (0, i)),
        ),
        out_shape=jax.ShapeDtypeStruct((rows, depth), jnp.bfloat16),
        cost_estimate=pl.CostEstimate(flops=0, bytes_accessed=6 * rows * depth, transcendentals=0),
        name="blend",
    )(scalars, hidden, routes.T, route_weight.T)


def mix_kernel(cells, scalars, *refs):
    halves, blends = refs[:2], refs[2 : 2 + cells]
    away_ref, keep_ref, combined = refs[2 + cells :]
    me, rep = scalars[0], scalars[1]
    span, chunk = halves[0].shape[0] // 2, blends[0].shape[0]
    mate = rep ^ 1

    @pl.when(pl.program_id(0) == 0)
    def _():
        for step in range(cells):
            target = me ^ step
            place = jnp.where(target == mate, 0, jnp.where(target == 3 - mate, 1, jnp.where(target == rep, 2, 3)))
            combined[pl.ds(pl.multiple_of(place * chunk, 16), chunk), :] = blends[step][...]

    total = jnp.zeros(combined.shape[:1] + away_ref.shape[1:], jnp.float32)
    for block in range(cells):
        restored = [
            (codes.astype(jnp.float32) * scale + zero).astype(jnp.bfloat16)
            for first in range(block % 2 * span, (block % 2 + 1) * span, SPAN)
            for g, codes, scale, zero in span_values(halves[block // 2], first, slice(None))
        ]
        total += jnp.dot(
            combined[:, pl.ds(pl.multiple_of((me ^ block) * span, SPAN), span)],
            jnp.concatenate(restored),
            preferred_element_type=jnp.float32,
        )
    away_ref[...] = total[: 2 * chunk].astype(away_ref.dtype)
    keep_ref[...] = total[2 * chunk :].astype(keep_ref.dtype)


def mix(scalars, halves, blends):
    cells = len(blends)
    rows, width = halves[0].shape
    chunk, depth = blends[0].shape
    tile = 256
    return pl.pallas_call(
        functools.partial(mix_kernel, cells),
        grid_spec=pltpu.PrefetchScalarGridSpec(
            num_scalar_prefetch=1,
            grid=(width // tile,),
            in_specs=[pl.BlockSpec((rows, tile), lambda i, scalars: (0, i))] * 2
            + [pl.BlockSpec((chunk, depth), lambda i, scalars: (0, 0))] * cells,
            out_specs=[pl.BlockSpec((2 * chunk, tile), lambda i, scalars: (0, i))] * 2,
            scratch_shapes=[
                pltpu.VMEM((cells * chunk, depth), jnp.bfloat16),
            ],
        ),
        out_shape=[jax.ShapeDtypeStruct((2 * chunk, width), jnp.bfloat16)] * 2,
        compiler_params=pltpu.CompilerParams(vmem_limit_bytes=VMEM_BYTES),
        cost_estimate=pl.CostEstimate(
            flops=2 * cells * chunk * depth * width,
            bytes_accessed=2 * (depth * width + cells * chunk * (depth + width)),
            transcendentals=0,
        ),
        name="mix",
    )(scalars, *halves, *blends)


def code_kernel(held, scalars, *refs):
    sources, out_ref, block = refs[:held], refs[-2], refs[-1]
    source = scalars[2 + pl.program_id(0)]
    for k in range(held):

        @pl.when(source == k)
        def _(k=k):
            block[...] = sources[k][...]

    @pl.when(source < held)
    def _():
        def piece(c, carry):
            lanes = pl.ds(pl.multiple_of(c * LANES, LANES), LANES)
            for first in range(0, out_ref.shape[2], SPAN):
                for g, codes, unused, unused in span_values(block, first, lanes):
                    out_ref[0, 0, first + g * GROUP : first + (g + 1) * GROUP, lanes] = codes
            return carry

        lax.fori_loop(0, out_ref.shape[3] // LANES, piece, 0)

    @pl.when(source == held)
    def _():
        out_ref[...] = jnp.zeros_like(out_ref)


def code(scalars, half, sources, so_far, depth):
    held = len(sources)
    rows, width = sources[0].shape
    tiles = 2 * TILES
    tile = rows // tiles

    def source_map(k):
        def index(slot, t, scalars):
            before = jnp.where((slot > 0) & (scalars[2] == k), tiles - 1, 0)
            return jnp.where(scalars[2 + slot] == k, t, before), 0

        return index

    def out_map(slot, t, scalars):
        return 0, slot, (scalars[0] ^ (2 * half + t // TILES)) * TILES + t % TILES, 0

    first = so_far is None
    return pl.pallas_call(
        functools.partial(code_kernel, held),
        grid_spec=pltpu.PrefetchScalarGridSpec(
            num_scalar_prefetch=1,
            grid=(MOST, tiles),
            in_specs=[pl.BlockSpec((tile, width), source_map(k)) for k in range(held)]
            + ([] if first else [pl.BlockSpec(memory_space=pl.ANY)]),
            out_specs=pl.BlockSpec((1, 1, tile, width), out_map),
            scratch_shapes=[pltpu.VMEM((tile, width), jnp.bfloat16)],
        ),
        out_shape=jax.ShapeDtypeStruct((1, MOST, depth, width), jnp.bfloat16),
        input_output_aliases={} if first else {1 + held: 0},
        compiler_params=pltpu.CompilerParams(vmem_limit_bytes=SMALL_BYTES),
        cost_estimate=pl.CostEstimate(
            flops=8 * MOST * rows * width, bytes_accessed=4 * MOST * rows * width * CODE_WEIGHT, transcendentals=0
        ),
        name=f"code_{half}",
    )(scalars, *sources, *([] if first else [so_far]))


def routed_body(cells, master, train_expert, rollout_owner, hidden, routes, route_weight):
    local_rows = master[0]
    reps = train_expert.shape[0]
    depth = cells * local_rows.shape[0]
    scalars = route(train_expert, rollout_owner)

    def swap(array, step):
        return lax.ppermute(array, CELL, [(c, c ^ step) for c in range(cells)])

    def to_owners(branch, *operands):
        return lax.switch(scalars[2 + MOST], [branch(rounds) for rounds in plans(reps)[0]], *operands)

    def moved(rounds, half):
        return tuple(lax.ppermute(half, "rep", pairs) for pairs in rounds)

    def near_moves(rounds):
        return lambda near, beyond, blend: (moved(rounds, near), swap(beyond, 2), swap(blend, 1))

    def far_moves(rounds):
        return lambda away, far: (lax.ppermute(away, "rep", [(r, r ^ 1) for r in range(reps)]), moved(rounds, far))

    blend = blend_rows(scalars, hidden, routes, route_weight)
    across = swap(blend, 2)
    local_rows, blend = lax.optimization_barrier((local_rows, blend))
    near, beyond = join(scalars, local_rows, swap(cut(scalars, local_rows, cells), 1), cells)
    near_arrived, far, beside = to_owners(near_moves, near, beyond, blend)
    across, far = lax.optimization_barrier((across, far))
    away, keep = mix(scalars, (near, far), [blend, beside, across, swap(across, 1)])
    brought, far_arrived = to_owners(far_moves, away, far)
    chunk = keep.shape[0] // 2

    def added(part, *terms):
        return sum(term[part].astype(jnp.float32) for term in terms)

    rest = lax.ppermute(
        added(slice(chunk, None), keep, brought).astype(jnp.bfloat16), "rep", [(r, reps - 1 - r) for r in range(reps)]
    )
    keep, brought, rest = lax.optimization_barrier((keep, brought, rest))
    mixed = added(slice(chunk), keep, brought, rest).astype(jnp.bfloat16)
    codes = code(scalars, 0, (near,) + near_arrived, None, depth)
    return code(scalars, 1, (far,) + far_arrived, codes, depth), mixed


def solution(mesh):
    in_specs = (
        P(("groups", "rep"), ("shard", "sub"), None),
        P(),
        P(),
        P(("groups", "shard", "sub"), None, None),
        P(("groups", "shard", "sub"), None),
        P(("groups", "shard", "sub"), None),
    )
    out_specs = (
        P(("groups", "rep"), None, None, ("shard", "sub")),
        P(("groups", "rep"), ("shard", "sub")),
    )
    cells = mesh.shape["shard"] * mesh.shape["sub"]
    reps = mesh.shape["rep"]

    def body(master, *rest):
        rows, columns = master.shape[1:]
        fits = reps == cells == 4 and rows % (4 * GROUP) == 0 and columns % (cells * 256) == 0
        if fits:
            return routed_body(cells, master, *rest)
        return general_body(master, *rest)

    return jax.shard_map(body, mesh=mesh, in_specs=in_specs, out_specs=out_specs, check_vma=False)
```

```python
import functools
import itertools

import jax
import jax.numpy as jnp
import numpy as np
from jax import lax
from jax.experimental import pallas as pl
from jax.experimental.pallas import tpu as pltpu
from jax.sharding import PartitionSpec as P

GROUP = 32
MOST = 2


LEVELS = 15.0
FLOOR = 0.02


def quantize(weights_block):
    row_count, col_count = weights_block.shape
    grouped = weights_block.reshape(row_count // GROUP, GROUP, col_count).astype(jnp.float32)
    lowest = jnp.min(grouped, axis=1)
    highest = jnp.max(grouped, axis=1)
    zero_point = lowest.astype(jnp.bfloat16)
    group_scale = (jnp.maximum(highest - lowest, FLOOR) / LEVELS).astype(jnp.bfloat16)
    code_values = (grouped - zero_point.astype(jnp.float32)[:, None, :]) / group_scale.astype(
        jnp.float32
    )[:, None, :]
    return (code_values.astype(jnp.bfloat16).reshape(row_count, col_count), group_scale, zero_point)


def restore(code_values, group_scale, zero_point):
    shape_full = code_values.shape
    grouped = code_values.reshape(
        shape_full[:-2] + (shape_full[-2] // GROUP, GROUP, shape_full[-1])
    ).astype(jnp.float32)
    restored = grouped * jnp.expand_dims(group_scale.astype(jnp.float32), -2) + jnp.expand_dims(
        zero_point.astype(jnp.float32), -2
    )
    return restored.astype(jnp.bfloat16).reshape(shape_full)


def local_slots(train_expert, rollout_owner, owner_index):
    total_experts = train_expert.shape[0]
    owners = rollout_owner[:, 0]
    labels = jnp.arange(total_experts, dtype=jnp.int32)
    same_owner = owners[:, None] == owners[None, :]
    ranking = jnp.sum((same_owner & (labels[None, :] < labels[:, None])).astype(jnp.int32), axis=1)
    own_mask = owners == owner_index
    chosen = []
    for slot_index in range(MOST):
        matched = own_mask & (ranking == slot_index)
        present = jnp.any(matched)
        expert_id = jnp.where(present, jnp.sum(jnp.where(matched, labels, 0)), -1)
        position = jnp.sum(jnp.where(train_expert == expert_id, labels, 0))
        chosen.append((expert_id, position, present))
    return chosen


def fold_select(chosen, selected, pieces, first_index):
    span = pieces[0].shape[0]
    result = []
    for member, held in zip(pieces, selected):
        layers = []
        for slot_index in range(MOST):
            expert_id, position, present = chosen[slot_index]
            inside = present & (position >= first_index) & (position < first_index + span)
            offset = jnp.clip(position, 0, span - 1)
            taken = lax.dynamic_index_in_dim(member, offset, 0, keepdims=False)
            layers.append(jnp.where(inside, taken, held[slot_index]))
        result.append(jnp.stack(layers))
    return tuple(result)


def general_body(master, train_expert, rollout_owner, hidden, routes, route_weight):
    local_rows = master[0]
    owner_index = lax.axis_index("rep")
    chosen = local_slots(train_expert, rollout_owner, owner_index)
    code_values, group_scale, zero_point = quantize(local_rows)
    relaid = (
        lax.all_to_all(code_values, ("shard", "sub"), split_axis=1, concat_axis=0, tiled=True),
        lax.all_to_all(group_scale, ("shard", "sub"), split_axis=1, concat_axis=0, tiled=True),
        lax.all_to_all(zero_point, ("shard", "sub"), split_axis=1, concat_axis=0, tiled=True),
    )
    start_slots = tuple((jnp.zeros((MOST,) + member.shape, member.dtype) for member in relaid))
    gathered = fold_select(
        chosen,
        start_slots,
        (
            lax.all_gather(relaid[0][None], "rep", axis=0, tiled=True),
            lax.all_gather(relaid[1][None], "rep", axis=0, tiled=True),
            lax.all_gather(relaid[2][None], "rep", axis=0, tiled=True),
        ),
        jnp.int32(0),
    )
    slot_codes = gathered[0]
    slot_values = restore(gathered[0], gathered[1], gathered[2])
    blended_list = []
    for slot_index in range(MOST):
        expert_id = chosen[slot_index][0]
        weight_here = jnp.where(routes == expert_id, route_weight, jnp.zeros((), jnp.float32))
        blended_list.append(jnp.sum(weight_here[:, :, None] * hidden, axis=1).astype(jnp.bfloat16))
    blended = jnp.stack(blended_list)
    all_blended = lax.all_gather(blended, ("shard", "sub"), axis=1, tiled=True)
    mixed = lax.psum_scatter(
        jnp.einsum("srf,sfd->rd", all_blended, slot_values, preferred_element_type=jnp.float32),
        "rep",
        scatter_dimension=0,
        tiled=True,
    ).astype(jnp.bfloat16)
    return (slot_codes[None], mixed)


CELL = ("shard", "sub")
VMEM_BYTES = 32 * 1024 * 1024
SMALL_BYTES = 16 * 1024 * 1024
ROUNDS = 2
TILES = 2
LANES = 256
MIX_TILE = 256
CODE_WEIGHT = 1


def moves(owners):
    return frozenset((p, owner) for p, owner in enumerate(owners) if owner != p)


def top_load(pairs, reps):
    return max(
        sum(low <= link < high for low, high in way)
        for way in ([(a, b) for a, b in pairs], [(b, a) for a, b in pairs])
        for link in range(reps - 1)
    )


def in_rounds(pairs):
    rounds = [[] for _ in range(ROUNDS)]

    def place(rest):
        if not rest:
            return True
        source, target = rest[0]
        for chosen in rounds:
            if all(source != a and target != b for a, b in chosen):
                chosen.append(rest[0])
                if place(rest[1:]):
                    return True
                chosen.pop()
        return False

    return rounds if place(sorted(pairs)) else None


@functools.lru_cache(maxsize=None)
def plans(reps):
    maps = [
        owners
        for owners in itertools.product(range(reps), repeat=reps)
        if max(owners.count(r) for r in range(reps)) <= MOST
    ]
    pairs = [(a, b) for a in range(reps) for b in range(reps) if a != b]
    chosen, table = [], np.zeros((reps**reps,), np.int32)
    loads = {owners: top_load(moves(owners), reps) for owners in maps}
    for load in sorted(set(loads.values()) | {1}):
        todo = sorted(owners for owners in maps if max(1, loads[owners]) == load)
        fitting = []
        for bits in range(1 << len(pairs)):
            subset = frozenset(pair for i, pair in enumerate(pairs) if bits >> i & 1)
            degrees = [sum(pair[side] == r for pair in subset) for side in (0, 1) for r in range(reps)]
            if max(degrees) <= ROUNDS and top_load(subset, reps) <= load:
                fitting.append(subset)
        while todo:
            best = max(fitting, key=lambda s: (sum(moves(o) <= s for o in todo), -len(s), sorted(s)))
            for owners in todo:
                if moves(owners) <= best:
                    table[sum(owner * reps**p for p, owner in enumerate(owners))] = len(chosen)
            todo = [o for o in todo if not moves(o) <= best]
            chosen.append(in_rounds(best))
    return chosen, table


def route_kernel(reps, train_ref, owner_ref, table_ref, round_ref, out_ref):
    rep = lax.axis_index("rep")
    cell = lax.axis_index(CELL)
    experts = [train_ref[p] for p in range(reps)]
    owners = [owner_ref[experts[p]] for p in range(reps)]
    number = sum(owners[p] * reps**p for p in range(reps))
    plan = table_ref[number]
    out_ref[0] = cell
    out_ref[1] = rep
    for slot in range(MOST):
        out_ref[2 + slot] = ROUNDS + 1
    for p in range(reps):
        rank = sum(
            ((owners[q] == owners[p]) & (experts[q] < experts[p])).astype(jnp.int32) for q in range(reps) if q != p
        )
        source = jnp.where(rep == p, 0, ROUNDS)
        for r in range(ROUNDS - 1):
            held = round_ref[(plan * ROUNDS + r) * reps + rep]
            source = jnp.where((rep != p) & (held == p), 1 + r, source)
        for slot in range(MOST):
            here = (owners[p] == rep) & (rank == slot)
            out_ref[2 + slot] = jnp.where(here, source, out_ref[2 + slot])
    out_ref[2 + MOST] = plan
    out_ref[3 + MOST] = train_ref[rep]


def route(train_expert, rollout_owner):
    reps = train_expert.shape[0]
    chosen, table = plans(reps)
    arrivals = np.full((len(chosen), ROUNDS, reps), -1, np.int32)
    for index, rounds in enumerate(chosen):
        for r, pairs in enumerate(rounds):
            for source, target in pairs:
                arrivals[index, r, target] = source
    smem = pl.BlockSpec(memory_space=pltpu.SMEM)
    return pl.pallas_call(
        functools.partial(route_kernel, reps),
        in_specs=[smem] * 4,
        out_specs=smem,
        out_shape=jax.ShapeDtypeStruct((4 + MOST,), jnp.int32),
        name="route",
    )(train_expert, rollout_owner[:, 0], jnp.asarray(table), jnp.asarray(arrivals.reshape(-1)))


SPAN = 8 * GROUP


def span_values(ref, first, lanes):
    rows = [pl.ds(first + g * GROUP, GROUP) for g in range(SPAN // GROUP)]
    lowest, highest = [], []
    for at in rows:
        block = ref[at, lanes]
        low = jnp.minimum(block[: GROUP // 2], block[GROUP // 2 :]).astype(jnp.float32)
        high = jnp.maximum(block[: GROUP // 2], block[GROUP // 2 :]).astype(jnp.float32)
        lowest.append(jnp.min(low, axis=0, keepdims=True))
        highest.append(jnp.max(high, axis=0, keepdims=True))
    lowest, highest = jnp.concatenate(lowest), jnp.concatenate(highest)
    scale = (jnp.maximum(highest - lowest, FLOOR) / LEVELS).astype(jnp.bfloat16).astype(jnp.float32)
    inverse = 1.0 / scale
    for g, at in enumerate(rows):
        zero = lowest[g : g + 1]
        codes = ((ref[at, lanes].astype(jnp.float32) - zero) * inverse[g : g + 1]).astype(jnp.bfloat16)
        yield g, codes, scale[g : g + 1], zero


def copy_kernel(scalars, *refs):
    count = 1 if len(refs) == 2 else 2
    for source_ref, out_ref in zip(refs[:count], refs[-count:]):
        out_ref[...] = source_ref[...]


def column_cost(rows, width):
    return pl.CostEstimate(flops=0, bytes_accessed=8 * rows * width, transcendentals=0)


def cut(scalars, master, cells):
    rows, width = master.shape[0], master.shape[1] // cells
    tile = rows // TILES
    return pl.pallas_call(
        copy_kernel,
        grid_spec=pltpu.PrefetchScalarGridSpec(
            num_scalar_prefetch=1,
            grid=(2, TILES),
            in_specs=[pl.BlockSpec((tile, width), lambda h, t, scalars: (t, scalars[0] ^ (1 + 2 * h)))],
            out_specs=[pl.BlockSpec((tile, width), lambda h, t, scalars: (h * TILES + t, 0))],
        ),
        out_shape=[jax.ShapeDtypeStruct((2 * rows, width), master.dtype)],
        compiler_params=pltpu.CompilerParams(vmem_limit_bytes=56 * 1024 * 1024),
        cost_estimate=column_cost(rows, width),
        name="cut",
    )(scalars, master)[0]


def join(scalars, master, other, cells):
    rows, width = master.shape[0], master.shape[1] // cells
    tile = rows // TILES
    shapes = [jax.ShapeDtypeStruct((2 * rows, width), master.dtype)] * 2
    own = pl.pallas_call(
        copy_kernel,
        grid_spec=pltpu.PrefetchScalarGridSpec(
            num_scalar_prefetch=1,
            grid=(TILES,),
            in_specs=[
                pl.BlockSpec((tile, width), lambda t, scalars: (t, scalars[0])),
                pl.BlockSpec((tile, width), lambda t, scalars: (t, scalars[0] ^ 2)),
            ],
            out_specs=[pl.BlockSpec((tile, width), lambda t, scalars: (t, 0))] * 2,
        ),
        out_shape=shapes,
        compiler_params=pltpu.CompilerParams(vmem_limit_bytes=SMALL_BYTES),
        cost_estimate=column_cost(rows, width),
        name="join_own",
    )(scalars, master, master)
    return pl.pallas_call(
        copy_kernel,
        grid_spec=pltpu.PrefetchScalarGridSpec(
            num_scalar_prefetch=1,
            grid=(TILES,),
            in_specs=[
                pl.BlockSpec((tile, width), lambda t, scalars: (t, 0)),
                pl.BlockSpec((tile, width), lambda t, scalars: (TILES + t, 0)),
                pl.BlockSpec(memory_space=pl.ANY),
                pl.BlockSpec(memory_space=pl.ANY),
            ],
            out_specs=[pl.BlockSpec((tile, width), lambda t, scalars: (TILES + t, 0))] * 2,
        ),
        out_shape=shapes,
        input_output_aliases={3: 0, 4: 1},
        compiler_params=pltpu.CompilerParams(vmem_limit_bytes=SMALL_BYTES),
        cost_estimate=column_cost(rows, width),
        name="join_other",
    )(scalars, other, other, *own)


def blend_kernel(scalars, hidden_ref, routes_ref, weights_ref, out_ref):
    weights = jnp.where(routes_ref[...] == scalars[3 + MOST], weights_ref[...], 0.0).T
    hidden = hidden_ref[...].astype(jnp.float32)
    total = weights[:, 0:1] * hidden[:, 0, :]
    for k in range(1, hidden.shape[1]):
        total += weights[:, k : k + 1] * hidden[:, k, :]
    out_ref[...] = total.astype(out_ref.dtype)


def blend_rows(scalars, hidden, routes, route_weight):
    rows, top, depth = hidden.shape
    tile = depth // TILES
    table = pl.BlockSpec((top, rows), lambda i, scalars: (0, 0))
    return pl.pallas_call(
        blend_kernel,
        grid_spec=pltpu.PrefetchScalarGridSpec(
            num_scalar_prefetch=1,
            grid=(TILES,),
            in_specs=[pl.BlockSpec((rows, top, tile), lambda i, scalars: (0, 0, i)), table, table],
            out_specs=pl.BlockSpec((rows, tile), lambda i, scalars: (0, i)),
        ),
        out_shape=jax.ShapeDtypeStruct((rows, depth), jnp.bfloat16),
        cost_estimate=pl.CostEstimate(flops=0, bytes_accessed=6 * rows * depth, transcendentals=0),
        name="blend",
    )(scalars, hidden, routes.T, route_weight.T)


def mix_kernel(cells, scalars, *refs):
    halves, blends = refs[:2], refs[2 : 2 + cells]
    outs, combined = refs[-5:-1], refs[-1]
    me, rep = scalars[0], scalars[1]
    span, chunk = halves[0].shape[0] // 2, blends[0].shape[0]
    mate = rep ^ 1

    @pl.when(pl.program_id(0) == 0)
    def _():
        for step in range(cells):
            target = me ^ step
            place = jnp.where(target == mate, 0, jnp.where(target == 3 - mate, 1, jnp.where(target == rep, 2, 3)))
            combined[pl.ds(pl.multiple_of(place * chunk, 16), chunk), :] = blends[step][...]

    total = jnp.zeros(combined.shape[:1] + outs[0].shape[1:], jnp.float32)
    for block in range(cells):
        restored = [
            (codes.astype(jnp.float32) * scale + zero).astype(jnp.bfloat16)
            for first in range(block % 2 * span, (block % 2 + 1) * span, SPAN)
            for g, codes, scale, zero in span_values(halves[block // 2], first, slice(None))
        ]
        total += jnp.dot(
            combined[:, pl.ds(pl.multiple_of((me ^ block) * span, SPAN), span)],
            jnp.concatenate(restored),
            preferred_element_type=jnp.float32,
        )
    for place, out_ref in zip((0, 2, 1, 3), outs):
        out_ref[...] = total[place * chunk : (place + 1) * chunk].astype(out_ref.dtype)


def mix(scalars, halves, blends, first, last, so_far):
    cells = len(blends)
    rows, width = halves[0].shape
    chunk, depth = blends[0].shape
    part = (last - first) * MIX_TILE
    block = (chunk, MIX_TILE)
    new = so_far is None
    return pl.pallas_call(
        functools.partial(mix_kernel, cells),
        grid_spec=pltpu.PrefetchScalarGridSpec(
            num_scalar_prefetch=1,
            grid=(last - first,),
            in_specs=[pl.BlockSpec((rows, MIX_TILE), lambda i, scalars: (0, first + i))] * 2
            + [pl.BlockSpec((chunk, depth), lambda i, scalars: (0, 0))] * cells
            + ([] if new else [pl.BlockSpec(memory_space=pl.ANY)] * 2),
            out_specs=[pl.BlockSpec(block, lambda i, scalars: (0, first + i))] * 2
            + [pl.BlockSpec(block, lambda i, scalars: (0, i))] * 2,
            scratch_shapes=[pltpu.VMEM((cells * chunk, depth), jnp.bfloat16)],
        ),
        out_shape=[jax.ShapeDtypeStruct((chunk, w), jnp.bfloat16) for w in (width, width, part, part)],
        input_output_aliases={} if new else {3 + cells: 0, 4 + cells: 1},
        compiler_params=pltpu.CompilerParams(vmem_limit_bytes=VMEM_BYTES),
        cost_estimate=pl.CostEstimate(
            flops=2 * cells * chunk * depth * part,
            bytes_accessed=2 * (depth * part + cells * chunk * (depth + part)),
            transcendentals=0,
        ),
        name=f"mix_{first}",
    )(scalars, *halves, *blends, *([] if new else so_far))


def code_kernel(held, scalars, *refs):
    sources, out_ref, block = refs[:held], refs[-2], refs[-1]
    source = scalars[2 + pl.program_id(0)]
    for k in range(held):

        @pl.when(source == k)
        def _(k=k):
            block[...] = sources[k][...]

    @pl.when(source < held)
    def _():
        def piece(c, carry):
            lanes = pl.ds(pl.multiple_of(c * LANES, LANES), LANES)
            for first in range(0, out_ref.shape[2], SPAN):
                for g, codes, unused, unused in span_values(block, first, lanes):
                    out_ref[0, 0, first + g * GROUP : first + (g + 1) * GROUP, lanes] = codes
            return carry

        lax.fori_loop(0, out_ref.shape[3] // LANES, piece, 0)

    @pl.when(source == held)
    def _():
        out_ref[...] = jnp.zeros_like(out_ref)


def code(scalars, half, sources, so_far, depth):
    held = len(sources)
    rows, width = sources[0].shape
    tiles = 2 * TILES
    tile = rows // tiles

    def source_map(k):
        def index(slot, t, scalars):
            before = jnp.where((slot > 0) & (scalars[2] == k), tiles - 1, 0)
            return jnp.where(scalars[2 + slot] == k, t, before), 0

        return index

    def out_map(slot, t, scalars):
        return 0, slot, (scalars[0] ^ (2 * half + t // TILES)) * TILES + t % TILES, 0

    first = so_far is None
    return pl.pallas_call(
        functools.partial(code_kernel, held),
        grid_spec=pltpu.PrefetchScalarGridSpec(
            num_scalar_prefetch=1,
            grid=(MOST, tiles),
            in_specs=[pl.BlockSpec((tile, width), source_map(k)) for k in range(held)]
            + ([] if first else [pl.BlockSpec(memory_space=pl.ANY)]),
            out_specs=pl.BlockSpec((1, 1, tile, width), out_map),
            scratch_shapes=[pltpu.VMEM((tile, width), jnp.bfloat16)],
        ),
        out_shape=jax.ShapeDtypeStruct((1, MOST, depth, width), jnp.bfloat16),
        input_output_aliases={} if first else {1 + held: 0},
        compiler_params=pltpu.CompilerParams(vmem_limit_bytes=SMALL_BYTES),
        cost_estimate=pl.CostEstimate(
            flops=8 * MOST * rows * width, bytes_accessed=4 * MOST * rows * width * CODE_WEIGHT, transcendentals=0
        ),
        name=f"code_{half}",
    )(scalars, *sources, *([] if first else [so_far]))


def routed_body(cells, master, train_expert, rollout_owner, hidden, routes, route_weight):
    local_rows = master[0]
    reps = train_expert.shape[0]
    depth = cells * local_rows.shape[0]
    scalars = route(train_expert, rollout_owner)

    def swap(array, step):
        return lax.ppermute(array, CELL, [(c, c ^ step) for c in range(cells)])

    def to_owners(branch, *operands):
        return lax.switch(scalars[2 + MOST], [branch(rounds) for rounds in plans(reps)[0]], *operands)

    def moved(rounds, half):
        return tuple(lax.ppermute(half, "rep", pairs) for pairs in rounds)

    def near_moves(rounds):
        return lambda near, beyond: (moved(rounds, near), swap(beyond, 2))

    def far_moves(rounds):
        def branch(far, blend):
            across = swap(blend, 2)
            return moved(rounds, far), [blend, swap(blend, 1), across, swap(across, 1)]

        return branch

    near, beyond = join(scalars, local_rows, swap(cut(scalars, local_rows, cells), 1), cells)
    blend = blend_rows(scalars, hidden, routes, route_weight)
    near_arrived, far = to_owners(near_moves, near, beyond)
    far_arrived, blends = to_owners(far_moves, far, blend)

    tiles = near.shape[1] // MIX_TILE
    mates, mirrored = [(r, r ^ 1) for r in range(reps)], [(r, reps - 1 - r) for r in range(reps)]
    middle = (tiles + 1) // 2
    *near_terms, to_far, far_terms = mix(scalars, (near, far), blends, middle, tiles, None)
    *near_terms, to_far_next, far_terms_next = mix(scalars, (near, far), blends, 0, middle, near_terms)

    def met(terms, sent):
        return (terms.astype(jnp.float32) + lax.ppermute(sent, "rep", mates).astype(jnp.float32)).astype(jnp.bfloat16)

    far_terms = met(far_terms, to_far)
    far_terms, to_far_next = lax.optimization_barrier((far_terms, to_far_next))
    far_terms_next = met(far_terms_next, to_far_next)
    near_terms, far_terms_next = lax.optimization_barrier((near_terms, far_terms_next))
    brought = [lax.ppermute(part, "rep", mirrored) for part in (far_terms_next, far_terms)]
    to_near, near_terms = near_terms
    near_terms = [near_terms, lax.ppermute(to_near, "rep", mates)]
    split = middle * MIX_TILE
    mixed = [
        sum(term.astype(jnp.float32) for term in [*(whole[:, at] for whole in near_terms), part]).astype(jnp.bfloat16)
        for at, part in zip((slice(split), slice(split, None)), brought)
    ]
    codes = code(scalars, 0, (near,) + near_arrived, None, depth)
    return code(scalars, 1, (far,) + far_arrived, codes, depth), jnp.concatenate(mixed, axis=1)


def solution(mesh):
    in_specs = (
        P(("groups", "rep"), ("shard", "sub"), None),
        P(),
        P(),
        P(("groups", "shard", "sub"), None, None),
        P(("groups", "shard", "sub"), None),
        P(("groups", "shard", "sub"), None),
    )
    out_specs = (
        P(("groups", "rep"), None, None, ("shard", "sub")),
        P(("groups", "rep"), ("shard", "sub")),
    )
    cells = mesh.shape["shard"] * mesh.shape["sub"]
    reps = mesh.shape["rep"]

    def body(master, *rest):
        rows, columns = master.shape[1:]
        fits = reps == cells == 4 and rows % (4 * GROUP) == 0 and columns % (cells * 256) == 0
        if fits:
            return routed_body(cells, master, *rest)
        return general_body(master, *rest)

    return jax.shard_map(body, mesh=mesh, in_specs=in_specs, out_specs=out_specs, check_vma=False)
```

```python
import functools
import itertools

import jax
import jax.numpy as jnp
import numpy as np
from jax import lax
from jax.experimental import pallas as pl
from jax.experimental.pallas import tpu as pltpu
from jax.sharding import PartitionSpec as P

GROUP = 32
MOST = 2


LEVELS = 15.0
FLOOR = 0.02


def quantize(weights_block):
    row_count, col_count = weights_block.shape
    grouped = weights_block.reshape(row_count // GROUP, GROUP, col_count).astype(jnp.float32)
    lowest = jnp.min(grouped, axis=1)
    highest = jnp.max(grouped, axis=1)
    zero_point = lowest.astype(jnp.bfloat16)
    group_scale = (jnp.maximum(highest - lowest, FLOOR) / LEVELS).astype(jnp.bfloat16)
    code_values = (grouped - zero_point.astype(jnp.float32)[:, None, :]) / group_scale.astype(
        jnp.float32
    )[:, None, :]
    return (code_values.astype(jnp.bfloat16).reshape(row_count, col_count), group_scale, zero_point)


def restore(code_values, group_scale, zero_point):
    shape_full = code_values.shape
    grouped = code_values.reshape(
        shape_full[:-2] + (shape_full[-2] // GROUP, GROUP, shape_full[-1])
    ).astype(jnp.float32)
    restored = grouped * jnp.expand_dims(group_scale.astype(jnp.float32), -2) + jnp.expand_dims(
        zero_point.astype(jnp.float32), -2
    )
    return restored.astype(jnp.bfloat16).reshape(shape_full)


def local_slots(train_expert, rollout_owner, owner_index):
    total_experts = train_expert.shape[0]
    owners = rollout_owner[:, 0]
    labels = jnp.arange(total_experts, dtype=jnp.int32)
    same_owner = owners[:, None] == owners[None, :]
    ranking = jnp.sum((same_owner & (labels[None, :] < labels[:, None])).astype(jnp.int32), axis=1)
    own_mask = owners == owner_index
    chosen = []
    for slot_index in range(MOST):
        matched = own_mask & (ranking == slot_index)
        present = jnp.any(matched)
        expert_id = jnp.where(present, jnp.sum(jnp.where(matched, labels, 0)), -1)
        position = jnp.sum(jnp.where(train_expert == expert_id, labels, 0))
        chosen.append((expert_id, position, present))
    return chosen


def fold_select(chosen, selected, pieces, first_index):
    span = pieces[0].shape[0]
    result = []
    for member, held in zip(pieces, selected):
        layers = []
        for slot_index in range(MOST):
            expert_id, position, present = chosen[slot_index]
            inside = present & (position >= first_index) & (position < first_index + span)
            offset = jnp.clip(position, 0, span - 1)
            taken = lax.dynamic_index_in_dim(member, offset, 0, keepdims=False)
            layers.append(jnp.where(inside, taken, held[slot_index]))
        result.append(jnp.stack(layers))
    return tuple(result)


def general_body(master, train_expert, rollout_owner, hidden, routes, route_weight):
    local_rows = master[0]
    owner_index = lax.axis_index("rep")
    chosen = local_slots(train_expert, rollout_owner, owner_index)
    code_values, group_scale, zero_point = quantize(local_rows)
    relaid = (
        lax.all_to_all(code_values, ("shard", "sub"), split_axis=1, concat_axis=0, tiled=True),
        lax.all_to_all(group_scale, ("shard", "sub"), split_axis=1, concat_axis=0, tiled=True),
        lax.all_to_all(zero_point, ("shard", "sub"), split_axis=1, concat_axis=0, tiled=True),
    )
    start_slots = tuple((jnp.zeros((MOST,) + member.shape, member.dtype) for member in relaid))
    gathered = fold_select(
        chosen,
        start_slots,
        (
            lax.all_gather(relaid[0][None], "rep", axis=0, tiled=True),
            lax.all_gather(relaid[1][None], "rep", axis=0, tiled=True),
            lax.all_gather(relaid[2][None], "rep", axis=0, tiled=True),
        ),
        jnp.int32(0),
    )
    slot_codes = gathered[0]
    slot_values = restore(gathered[0], gathered[1], gathered[2])
    blended_list = []
    for slot_index in range(MOST):
        expert_id = chosen[slot_index][0]
        weight_here = jnp.where(routes == expert_id, route_weight, jnp.zeros((), jnp.float32))
        blended_list.append(jnp.sum(weight_here[:, :, None] * hidden, axis=1).astype(jnp.bfloat16))
    blended = jnp.stack(blended_list)
    all_blended = lax.all_gather(blended, ("shard", "sub"), axis=1, tiled=True)
    mixed = lax.psum_scatter(
        jnp.einsum("srf,sfd->rd", all_blended, slot_values, preferred_element_type=jnp.float32),
        "rep",
        scatter_dimension=0,
        tiled=True,
    ).astype(jnp.bfloat16)
    return (slot_codes[None], mixed)


CELL = ("shard", "sub")
VMEM_BYTES = 32 * 1024 * 1024
SMALL_BYTES = 16 * 1024 * 1024
ROUNDS = 2
TILES = 2
LANES = 256
MIX_TILE = 256
CODE_WEIGHT = 1


def moves(owners):
    return frozenset((p, owner) for p, owner in enumerate(owners) if owner != p)


def top_load(pairs, reps):
    return max(
        sum(low <= link < high for low, high in way)
        for way in ([(a, b) for a, b in pairs], [(b, a) for a, b in pairs])
        for link in range(reps - 1)
    )


def in_rounds(pairs):
    rounds = [[] for _ in range(ROUNDS)]

    def place(rest):
        if not rest:
            return True
        source, target = rest[0]
        for chosen in rounds:
            if all(source != a and target != b for a, b in chosen):
                chosen.append(rest[0])
                if place(rest[1:]):
                    return True
                chosen.pop()
        return False

    return rounds if place(sorted(pairs)) else None


@functools.lru_cache(maxsize=None)
def plans(reps):
    maps = [
        owners
        for owners in itertools.product(range(reps), repeat=reps)
        if max(owners.count(r) for r in range(reps)) <= MOST
    ]
    pairs = [(a, b) for a in range(reps) for b in range(reps) if a != b]
    chosen, table = [], np.zeros((reps**reps,), np.int32)
    loads = {owners: top_load(moves(owners), reps) for owners in maps}
    for load in sorted(set(loads.values()) | {1}):
        todo = sorted(owners for owners in maps if max(1, loads[owners]) == load)
        fitting = []
        for bits in range(1 << len(pairs)):
            subset = frozenset(pair for i, pair in enumerate(pairs) if bits >> i & 1)
            degrees = [sum(pair[side] == r for pair in subset) for side in (0, 1) for r in range(reps)]
            if max(degrees) <= ROUNDS and top_load(subset, reps) <= load:
                fitting.append(subset)
        while todo:
            best = max(fitting, key=lambda s: (sum(moves(o) <= s for o in todo), -len(s), sorted(s)))
            for owners in todo:
                if moves(owners) <= best:
                    table[sum(owner * reps**p for p, owner in enumerate(owners))] = len(chosen)
            todo = [o for o in todo if not moves(o) <= best]
            chosen.append(in_rounds(best))
    return chosen, table


def route_kernel(reps, train_ref, owner_ref, table_ref, round_ref, out_ref):
    rep = lax.axis_index("rep")
    cell = lax.axis_index(CELL)
    experts = [train_ref[p] for p in range(reps)]
    owners = [owner_ref[experts[p]] for p in range(reps)]
    number = sum(owners[p] * reps**p for p in range(reps))
    plan = table_ref[number]
    out_ref[0] = cell
    out_ref[1] = rep
    for slot in range(MOST):
        out_ref[2 + slot] = ROUNDS + 1
    for p in range(reps):
        rank = sum(
            ((owners[q] == owners[p]) & (experts[q] < experts[p])).astype(jnp.int32) for q in range(reps) if q != p
        )
        source = jnp.where(rep == p, 0, ROUNDS)
        for r in range(ROUNDS - 1):
            held = round_ref[(plan * ROUNDS + r) * reps + rep]
            source = jnp.where((rep != p) & (held == p), 1 + r, source)
        for slot in range(MOST):
            here = (owners[p] == rep) & (rank == slot)
            out_ref[2 + slot] = jnp.where(here, source, out_ref[2 + slot])
    out_ref[2 + MOST] = plan
    out_ref[3 + MOST] = train_ref[rep]


def route(train_expert, rollout_owner):
    reps = train_expert.shape[0]
    chosen, table = plans(reps)
    arrivals = np.full((len(chosen), ROUNDS, reps), -1, np.int32)
    for index, rounds in enumerate(chosen):
        for r, pairs in enumerate(rounds):
            for source, target in pairs:
                arrivals[index, r, target] = source
    smem = pl.BlockSpec(memory_space=pltpu.SMEM)
    return pl.pallas_call(
        functools.partial(route_kernel, reps),
        in_specs=[smem] * 4,
        out_specs=smem,
        out_shape=jax.ShapeDtypeStruct((4 + MOST,), jnp.int32),
        name="route",
    )(train_expert, rollout_owner[:, 0], jnp.asarray(table), jnp.asarray(arrivals.reshape(-1)))


SPAN = 8 * GROUP


def span_values(ref, first, lanes):
    rows = [pl.ds(first + g * GROUP, GROUP) for g in range(SPAN // GROUP)]
    lowest, highest = [], []
    for at in rows:
        block = ref[at, lanes]
        low = jnp.minimum(block[: GROUP // 2], block[GROUP // 2 :]).astype(jnp.float32)
        high = jnp.maximum(block[: GROUP // 2], block[GROUP // 2 :]).astype(jnp.float32)
        lowest.append(jnp.min(low, axis=0, keepdims=True))
        highest.append(jnp.max(high, axis=0, keepdims=True))
    lowest, highest = jnp.concatenate(lowest), jnp.concatenate(highest)
    scale = (jnp.maximum(highest - lowest, FLOOR) / LEVELS).astype(jnp.bfloat16).astype(jnp.float32)
    inverse = 1.0 / scale
    for g, at in enumerate(rows):
        zero = lowest[g : g + 1]
        codes = ((ref[at, lanes].astype(jnp.float32) - zero) * inverse[g : g + 1]).astype(jnp.bfloat16)
        yield g, codes, scale[g : g + 1], zero


def copy_kernel(scalars, *refs):
    count = 1 if len(refs) == 2 else 2
    for source_ref, out_ref in zip(refs[:count], refs[-count:]):
        out_ref[...] = source_ref[...]


def column_cost(rows, width):
    return pl.CostEstimate(flops=0, bytes_accessed=8 * rows * width, transcendentals=0)


def cut(scalars, master, cells):
    rows, width = master.shape[0], master.shape[1] // cells
    tile = rows
    return pl.pallas_call(
        copy_kernel,
        grid_spec=pltpu.PrefetchScalarGridSpec(
            num_scalar_prefetch=1,
            grid=(2, 1),
            in_specs=[pl.BlockSpec((tile, width), lambda h, t, scalars: (t, scalars[0] ^ (1 + 2 * h)))],
            out_specs=[pl.BlockSpec((tile, width), lambda h, t, scalars: (h + t, 0))],
        ),
        out_shape=[jax.ShapeDtypeStruct((2 * rows, width), master.dtype)],
        compiler_params=pltpu.CompilerParams(vmem_limit_bytes=56 * 1024 * 1024),
        cost_estimate=column_cost(rows, width),
        name="cut",
    )(scalars, master)[0]


def join(scalars, master, other, cells):
    rows, width = master.shape[0], master.shape[1] // cells
    tile = rows // TILES
    shapes = [jax.ShapeDtypeStruct((2 * rows, width), master.dtype)] * 2
    own = pl.pallas_call(
        copy_kernel,
        grid_spec=pltpu.PrefetchScalarGridSpec(
            num_scalar_prefetch=1,
            grid=(TILES,),
            in_specs=[
                pl.BlockSpec((tile, width), lambda t, scalars: (t, scalars[0])),
                pl.BlockSpec((tile, width), lambda t, scalars: (t, scalars[0] ^ 2)),
            ],
            out_specs=[pl.BlockSpec((tile, width), lambda t, scalars: (t, 0))] * 2,
        ),
        out_shape=shapes,
        compiler_params=pltpu.CompilerParams(vmem_limit_bytes=SMALL_BYTES),
        cost_estimate=column_cost(rows, width),
        name="join_own",
    )(scalars, master, master)
    return pl.pallas_call(
        copy_kernel,
        grid_spec=pltpu.PrefetchScalarGridSpec(
            num_scalar_prefetch=1,
            grid=(TILES,),
            in_specs=[
                pl.BlockSpec((tile, width), lambda t, scalars: (t, 0)),
                pl.BlockSpec((tile, width), lambda t, scalars: (TILES + t, 0)),
                pl.BlockSpec(memory_space=pl.ANY),
                pl.BlockSpec(memory_space=pl.ANY),
            ],
            out_specs=[pl.BlockSpec((tile, width), lambda t, scalars: (TILES + t, 0))] * 2,
        ),
        out_shape=shapes,
        input_output_aliases={3: 0, 4: 1},
        compiler_params=pltpu.CompilerParams(vmem_limit_bytes=SMALL_BYTES),
        cost_estimate=column_cost(rows, width),
        name="join_other",
    )(scalars, other, other, *own)


def blend_kernel(scalars, hidden_ref, routes_ref, weights_ref, out_ref):
    weights = jnp.where(routes_ref[...] == scalars[3 + MOST], weights_ref[...], 0.0).T
    hidden = hidden_ref[...].astype(jnp.float32)
    total = weights[:, 0:1] * hidden[:, 0, :]
    for k in range(1, hidden.shape[1]):
        total += weights[:, k : k + 1] * hidden[:, k, :]
    out_ref[...] = total.astype(out_ref.dtype)


def blend_rows(scalars, hidden, routes, route_weight):
    rows, top, depth = hidden.shape
    tile = depth // TILES
    table = pl.BlockSpec((top, rows), lambda i, scalars: (0, 0))
    return pl.pallas_call(
        blend_kernel,
        grid_spec=pltpu.PrefetchScalarGridSpec(
            num_scalar_prefetch=1,
            grid=(TILES,),
            in_specs=[pl.BlockSpec((rows, top, tile), lambda i, scalars: (0, 0, i)), table, table],
            out_specs=pl.BlockSpec((rows, tile), lambda i, scalars: (0, i)),
        ),
        out_shape=jax.ShapeDtypeStruct((rows, depth), jnp.bfloat16),
        cost_estimate=pl.CostEstimate(flops=0, bytes_accessed=6 * rows * depth, transcendentals=0),
        name="blend",
    )(scalars, hidden, routes.T, route_weight.T)


def mix_kernel(cells, scalars, *refs):
    halves, blends = refs[:2], refs[2 : 2 + cells]
    outs, combined = refs[-5:-1], refs[-1]
    me, rep = scalars[0], scalars[1]
    span, chunk = halves[0].shape[0] // 2, blends[0].shape[0]
    mate = rep ^ 1

    @pl.when(pl.program_id(0) == 0)
    def _():
        for step in range(cells):
            target = me ^ step
            place = jnp.where(target == mate, 0, jnp.where(target == 3 - mate, 1, jnp.where(target == rep, 2, 3)))
            combined[pl.ds(pl.multiple_of(place * chunk, 16), chunk), :] = blends[step][...]

    total = jnp.zeros(combined.shape[:1] + outs[0].shape[1:], jnp.float32)
    for block in range(cells):
        restored = [
            (codes.astype(jnp.float32) * scale + zero).astype(jnp.bfloat16)
            for first in range(block % 2 * span, (block % 2 + 1) * span, SPAN)
            for g, codes, scale, zero in span_values(halves[block // 2], first, slice(None))
        ]
        total += jnp.dot(
            combined[:, pl.ds(pl.multiple_of((me ^ block) * span, SPAN), span)],
            jnp.concatenate(restored),
            preferred_element_type=jnp.float32,
        )
    for place, out_ref in zip((0, 2, 1, 3), outs):
        out_ref[...] = total[place * chunk : (place + 1) * chunk].astype(out_ref.dtype)


def mix(scalars, halves, blends, first, last, so_far):
    cells = len(blends)
    rows, width = halves[0].shape
    chunk, depth = blends[0].shape
    part = (last - first) * MIX_TILE
    block = (chunk, MIX_TILE)
    new = so_far is None
    return pl.pallas_call(
        functools.partial(mix_kernel, cells),
        grid_spec=pltpu.PrefetchScalarGridSpec(
            num_scalar_prefetch=1,
            grid=(last - first,),
            in_specs=[pl.BlockSpec((rows, MIX_TILE), lambda i, scalars: (0, first + i))] * 2
            + [pl.BlockSpec((chunk, depth), lambda i, scalars: (0, 0))] * cells
            + ([] if new else [pl.BlockSpec(memory_space=pl.ANY)] * 2),
            out_specs=[pl.BlockSpec(block, lambda i, scalars: (0, first + i))] * 2
            + [pl.BlockSpec(block, lambda i, scalars: (0, i))] * 2,
            scratch_shapes=[pltpu.VMEM((cells * chunk, depth), jnp.bfloat16)],
        ),
        out_shape=[jax.ShapeDtypeStruct((chunk, w), jnp.bfloat16) for w in (width, width, part, part)],
        input_output_aliases={} if new else {3 + cells: 0, 4 + cells: 1},
        compiler_params=pltpu.CompilerParams(vmem_limit_bytes=VMEM_BYTES),
        cost_estimate=pl.CostEstimate(
            flops=2 * cells * chunk * depth * part,
            bytes_accessed=2 * (depth * part + cells * chunk * (depth + part)),
            transcendentals=0,
        ),
        name=f"mix_{first}",
    )(scalars, *halves, *blends, *([] if new else so_far))


def code_kernel(held, scalars, *refs):
    sources, out_ref, block = refs[:held], refs[-2], refs[-1]
    source = scalars[2 + pl.program_id(0)]
    for k in range(held):

        @pl.when(source == k)
        def _(k=k):
            block[...] = sources[k][...]

    @pl.when(source < held)
    def _():
        def piece(c, carry):
            lanes = pl.ds(pl.multiple_of(c * LANES, LANES), LANES)
            for first in range(0, out_ref.shape[2], SPAN):
                for g, codes, unused, unused in span_values(block, first, lanes):
                    out_ref[0, 0, first + g * GROUP : first + (g + 1) * GROUP, lanes] = codes
            return carry

        lax.fori_loop(0, out_ref.shape[3] // LANES, piece, 0)

    @pl.when(source == held)
    def _():
        out_ref[...] = jnp.zeros_like(out_ref)


def code(scalars, half, sources, so_far, depth):
    held = len(sources)
    rows, width = sources[0].shape
    tiles = 2 * TILES
    tile = rows // tiles

    def source_map(k):
        def index(slot, t, scalars):
            before = jnp.where((slot > 0) & (scalars[2] == k), tiles - 1, 0)
            return jnp.where(scalars[2 + slot] == k, t, before), 0

        return index

    def out_map(slot, t, scalars):
        return 0, slot, (scalars[0] ^ (2 * half + t // TILES)) * TILES + t % TILES, 0

    first = so_far is None
    return pl.pallas_call(
        functools.partial(code_kernel, held),
        grid_spec=pltpu.PrefetchScalarGridSpec(
            num_scalar_prefetch=1,
            grid=(MOST, tiles),
            in_specs=[pl.BlockSpec((tile, width), source_map(k)) for k in range(held)]
            + ([] if first else [pl.BlockSpec(memory_space=pl.ANY)]),
            out_specs=pl.BlockSpec((1, 1, tile, width), out_map),
            scratch_shapes=[pltpu.VMEM((tile, width), jnp.bfloat16)],
        ),
        out_shape=jax.ShapeDtypeStruct((1, MOST, depth, width), jnp.bfloat16),
        input_output_aliases={} if first else {1 + held: 0},
        compiler_params=pltpu.CompilerParams(vmem_limit_bytes=SMALL_BYTES),
        cost_estimate=pl.CostEstimate(
            flops=8 * MOST * rows * width, bytes_accessed=4 * MOST * rows * width * CODE_WEIGHT, transcendentals=0
        ),
        name=f"code_{half}",
    )(scalars, *sources, *([] if first else [so_far]))


def routed_body(cells, master, train_expert, rollout_owner, hidden, routes, route_weight):
    local_rows = master[0]
    reps = train_expert.shape[0]
    depth = cells * local_rows.shape[0]
    scalars = route(train_expert, rollout_owner)

    def swap(array, step):
        return lax.ppermute(array, CELL, [(c, c ^ step) for c in range(cells)])

    def to_owners(branch, *operands):
        return lax.switch(scalars[2 + MOST], [branch(rounds) for rounds in plans(reps)[0]], *operands)

    def moved(rounds, half):
        return tuple(lax.ppermute(half, "rep", pairs) for pairs in rounds)

    def near_moves(rounds):
        return lambda near, beyond: (moved(rounds, near), swap(beyond, 2))

    def far_moves(rounds):
        def branch(far, blend):
            across = swap(blend, 2)
            return moved(rounds, far), [blend, swap(blend, 1), across, swap(across, 1)]

        return branch

    near, beyond = join(scalars, local_rows, swap(cut(scalars, local_rows, cells), 1), cells)
    blend = blend_rows(scalars, hidden, routes, route_weight)
    near_arrived, far = to_owners(near_moves, near, beyond)
    far_arrived, blends = to_owners(far_moves, far, blend)

    tiles = near.shape[1] // MIX_TILE
    mates, mirrored = [(r, r ^ 1) for r in range(reps)], [(r, reps - 1 - r) for r in range(reps)]
    middle = (tiles + 1) // 2
    *near_terms, to_far, far_terms = mix(scalars, (near, far), blends, middle, tiles, None)
    *near_terms, to_far_next, far_terms_next = mix(scalars, (near, far), blends, 0, middle, near_terms)

    def met(terms, sent):
        return (terms.astype(jnp.float32) + lax.ppermute(sent, "rep", mates).astype(jnp.float32)).astype(jnp.bfloat16)

    far_terms = met(far_terms, to_far)
    far_terms, to_far_next = lax.optimization_barrier((far_terms, to_far_next))
    far_terms_next = met(far_terms_next, to_far_next)
    near_terms, far_terms_next = lax.optimization_barrier((near_terms, far_terms_next))
    brought = [lax.ppermute(part, "rep", mirrored) for part in (far_terms_next, far_terms)]
    to_near, near_terms = near_terms
    near_terms = [near_terms, lax.ppermute(to_near, "rep", mates)]
    split = middle * MIX_TILE
    mixed = [
        sum(term.astype(jnp.float32) for term in [*(whole[:, at] for whole in near_terms), part]).astype(jnp.bfloat16)
        for at, part in zip((slice(split), slice(split, None)), brought)
    ]
    codes = code(scalars, 0, (near,) + near_arrived, None, depth)
    return code(scalars, 1, (far,) + far_arrived, codes, depth), jnp.concatenate(mixed, axis=1)


def solution(mesh):
    in_specs = (
        P(("groups", "rep"), ("shard", "sub"), None),
        P(),
        P(),
        P(("groups", "shard", "sub"), None, None),
        P(("groups", "shard", "sub"), None),
        P(("groups", "shard", "sub"), None),
    )
    out_specs = (
        P(("groups", "rep"), None, None, ("shard", "sub")),
        P(("groups", "rep"), ("shard", "sub")),
    )
    cells = mesh.shape["shard"] * mesh.shape["sub"]
    reps = mesh.shape["rep"]

    def body(master, *rest):
        rows, columns = master.shape[1:]
        fits = reps == cells == 4 and rows % (4 * GROUP) == 0 and columns % (cells * 256) == 0
        if fits:
            return routed_body(cells, master, *rest)
        return general_body(master, *rest)

    return jax.shard_map(body, mesh=mesh, in_specs=in_specs, out_specs=out_specs, check_vma=False)
```
